128 devices in a mesh: dp: 32 (over x, z, core), ctx: 4 (over y).
Axes of the slice: x: 4, y: 4, z: 4, core: 2. Of those that a mesh axis runs over, the one named last changes fastest.
Arguments:
- activations: bfloat16 [32, 512, 1152], P('dp', 'ctx'), may hold values from -6 to 6
- cotangent: bfloat16 [32, 512, 1152], P('dp', 'ctx'), may hold values from -6 to 6
- segments: int32 [32, 512], P('dp'), may hold values from 0 to 4, as said below
- in_gain: bfloat16 [1152], P(('dp', 'ctx')), may hold values from -0.5 to 0.5
- query_gain: bfloat16 [256], P(('dp', 'ctx')), may hold values from -0.5 to 0.5
- key_gain: bfloat16 [256], P(('dp', 'ctx')), may hold values from -0.5 to 0.5
- post_attn_gain: bfloat16 [1152], P(('dp', 'ctx')), may hold values from -0.5 to 0.5
- pre_ff_gain: bfloat16 [1152], P(('dp', 'ctx')), may hold values from -0.5 to 0.5
- post_ff_gain: bfloat16 [1152], P(('dp', 'ctx')), may hold values from -0.5 to 0.5
- w_query: bfloat16 [1152, 1024], P(('dp', 'ctx')), may hold values from -0.1875 to 0.1875
- w_key: bfloat16 [1152, 256], P(('dp', 'ctx')), may hold values from -0.1875 to 0.1875
- w_value: bfloat16 [1152, 256], P(('dp', 'ctx')), may hold values from -0.1875 to 0.1875
- w_out: bfloat16 [1024, 1152], P(('dp', 'ctx')), may hold values from -0.1875 to 0.1875
- w_gate: bfloat16 [1152, 6912], P(('dp', 'ctx')), may hold values from -0.1875 to 0.1875
- w_up: bfloat16 [1152, 6912], P(('dp', 'ctx')), may hold values from -0.1875 to 0.1875
- w_down: bfloat16 [6912, 1152], P(('dp', 'ctx')), may hold values from -0.078125 to 0.078125
Outputs:
- output: bfloat16 [32, 512, 1152], P('dp', 'ctx')
- input_grad: float32 [32, 512, 1152], P('dp', 'ctx')
- in_gain_grad: float32 [1152], P(('dp', 'ctx'))
- query_gain_grad: float32 [256], P(('dp', 'ctx'))
- key_gain_grad: float32 [256], P(('dp', 'ctx'))
- post_attn_gain_grad: float32 [1152], P(('dp', 'ctx'))
- pre_ff_gain_grad: float32 [1152], P(('dp', 'ctx'))
- post_ff_gain_grad: float32 [1152], P(('dp', 'ctx'))
- w_query_grad: float32 [1152, 1024], P(('dp', 'ctx'))
- w_key_grad: float32 [1152, 256], P(('dp', 'ctx'))
- w_value_grad: float32 [1152, 256], P(('dp', 'ctx'))
- w_out_grad: float32 [1024, 1152], P(('dp', 'ctx'))
- w_gate_grad: float32 [1152, 6912], P(('dp', 'ctx'))
- w_up_grad: float32 [1152, 6912], P(('dp', 'ctx'))
- w_down_grad: float32 [6912, 1152], P(('dp', 'ctx'))
The draws below stay inside these ranges and needn't reach their ends.
Inputs may be any that keep to these rules, and one draw needn't show every extreme that they name: `segments`: segment numbers never fall along a sequence and may skip values; in every sequence one document begins within the first 64 tokens and ends within the last 64 tokens.
All inputs are finite; a program needn't handle non-finite values.
Results may differ from the reference program's by a relative error of at most 0.035.
Values may be sent and summed in bfloat16 or wider, within the bound.
No kernel may reach another device: no remote copies, remote signals or barrier semaphores. Data moves between devices by JAX's collectives and lax.ppermute only.
A program may use at most 256 MiB of HBM per device.

```python
import math
import jax
import jax.numpy as jnp
from jax import lax

D = 1152
H = 4
HD = 256
FF = 6912
TOK_DEV = 128
LENGTH = 512
SEQS = 32


def draw_segments(key, part):
    base = jax.random.fold_in(key, 11)
    keys = jax.random.split(base, 4)
    half_span = TOK_DEV // 2
    first_cut = jax.random.randint(keys[0], (SEQS, 1), 1, half_span + 1)
    early_cut = jax.random.randint(keys[1], (SEQS, 1), 1, half_span + 1)
    last_cut = jax.random.randint(keys[2], (SEQS, 1), LENGTH - half_span, LENGTH)
    late_cut = jax.random.randint(keys[3], (SEQS, 1), LENGTH - half_span, LENGTH + 1)
    places = jnp.arange(LENGTH, dtype=jnp.int32)[None, :]
    counted = (places >= first_cut).astype(jnp.int32) + (places >= early_cut).astype(jnp.int32)
    counted = counted + (places >= last_cut).astype(jnp.int32) + (places >= late_cut).astype(jnp.int32)
    return counted


def with_spikes(array, stream_key, source, target, parts, factor):
    owner, partner = [(jnp.arange(array.shape[position]) // (array.shape[position] // parts)).reshape([-1 if axis == position else 1 for axis in range(array.ndim)]) for position in (source, target)]
    chosen = jax.random.permutation(stream_key, parts)[partner]
    strong = (owner == chosen) | (owner == (partner + parts // 2) % parts)
    return jnp.where(strong, factor * array, array)


def block_levels(own_key, extent, cuts, low, largest):
    level, own = 1.0, jax.random.fold_in(own_key, 6)
    for position, parts in cuts:
        draws = jnp.exp(jax.random.uniform(jax.random.fold_in(own, position), (parts,), jnp.float32, low / len(cuts), largest / len(cuts)))
        level = level * jnp.repeat(draws, extent[position] // parts).reshape([-1 if axis == position else 1 for axis in range(len(extent))])
    return level


def normal_values(stream_key, extent, scale, most, shards=(), kind=jnp.bfloat16):
    array = scale * jax.random.normal(stream_key, extent, jnp.float32)
    if shards:
        array = array * block_levels(stream_key, extent, shards, -0.22, 0.18)
    return jnp.clip(array, -most, most).astype(kind)


def gaussian_with(own_key, dims, deviation, limit, pieces, heavy, kind=jnp.bfloat16):
    drawn = deviation * jax.random.normal(own_key, dims, jnp.float32)
    if pieces:
        drawn = drawn * block_levels(own_key, dims, pieces, -0.22, 0.18)
    return jnp.clip(with_spikes(drawn, jax.random.fold_in(own_key, 3), *heavy), -limit, limit).astype(kind)


def setup_inputs(seed: int = 0) -> dict:
    splits = jax.random.split(jax.random.key(seed), 17)
    activations = normal_values(splits[0], (SEQS, LENGTH, D), 1.0, 6.0, ((0, 32), (1, 4)))
    cotangent = gaussian_with(splits[1], (SEQS, LENGTH, D), 1.0, 6.0, ((0, 32), (1, 4)), (0, 2, 32, 2.75))
    segments = draw_segments(jax.random.fold_in(splits[16], 71), 0)
    in_gain = jnp.clip(jax.random.uniform(splits[3], (D,), jnp.float32, -0.5, 0.5) * block_levels(splits[3], (D,), ((0, 128),), -0.4, 0.0), -0.5, 0.5).astype(jnp.bfloat16)
    query_gain = jnp.clip(jax.random.uniform(splits[4], (HD,), jnp.float32, -0.5, 0.5) * block_levels(splits[4], (HD,), ((0, 128),), -0.4, 0.0), -0.5, 0.5).astype(jnp.bfloat16)
    key_gain = jnp.clip(jax.random.uniform(splits[5], (HD,), jnp.float32, -0.5, 0.5) * block_levels(splits[5], (HD,), ((0, 128),), -0.4, 0.0), -0.5, 0.5).astype(jnp.bfloat16)
    post_attn_gain = jnp.clip(jax.random.uniform(splits[6], (D,), jnp.float32, -0.5, 0.5) * block_levels(splits[6], (D,), ((0, 128),), -0.4, 0.0), -0.5, 0.5).astype(jnp.bfloat16)
    pre_ff_gain = jnp.clip(jax.random.uniform(splits[7], (D,), jnp.float32, -0.5, 0.5) * block_levels(splits[7], (D,), ((0, 128),), -0.4, 0.0), -0.5, 0.5).astype(jnp.bfloat16)
    post_ff_gain = jnp.clip(jax.random.uniform(splits[8], (D,), jnp.float32, -0.5, 0.5) * block_levels(splits[8], (D,), ((0, 128),), -0.4, 0.0), -0.5, 0.5).astype(jnp.bfloat16)
    w_query = normal_values(splits[9], (D, H * HD), D ** -0.5, 0.1875, ((0, 128),))
    w_key = normal_values(splits[10], (D, HD), D ** -0.5, 0.1875, ((0, 128),))
    w_value = normal_values(splits[11], (D, HD), D ** -0.5, 0.1875, ((0, 128),))
    w_out = normal_values(splits[12], (H * HD, D), (H * HD) ** -0.5, 0.1875, ((0, 128),))
    w_gate = normal_values(splits[13], (D, FF), D ** -0.5, 0.1875, ((0, 128),))
    w_up = normal_values(splits[14], (D, FF), D ** -0.5, 0.1875, ((0, 128),))
    w_down = normal_values(splits[15], (FF, D), FF ** -0.5, 0.078125, ((0, 128),))
    return {"activations": activations, "cotangent": cotangent, "segments": segments, "in_gain": in_gain, "query_gain": query_gain, "key_gain": key_gain, "post_attn_gain": post_attn_gain, "pre_ff_gain": pre_ff_gain, "post_ff_gain": post_ff_gain, "w_query": w_query, "w_key": w_key, "w_value": w_value, "w_out": w_out, "w_gate": w_gate, "w_up": w_up, "w_down": w_down}


@jax.custom_vjp
def low(v):
    return lax.optimization_barrier(v.astype(jnp.bfloat16)).astype(jnp.float32)

@jax.custom_vjp
def low_back(v):
    return v

def low_keep(v):
    return (low(v), None)

def low_pass(kept, grad):
    return (grad,)

def back_keep(v):
    return (v, None)

def back_low(kept, grad):
    return (low(grad),)
low.defvjp(low_keep, low_pass)
low_back.defvjp(back_keep, back_low)
norm_eps = 1e-06
rope_base = 1000000.0
score_scale = 0.0625
far_below = -1e+30

def rms_norm(values, gain):
    factor = lax.rsqrt(lax.optimization_barrier(jnp.mean(values * values, axis=-1, keepdims=True)) + norm_eps)
    return values * factor * (1.0 + gain)

def rotate(values, cosine, sine):
    half_dim = values.shape[-1] // 2
    first_half = values[..., :half_dim]
    second_half = values[..., half_dim:]
    return jnp.concatenate([first_half * cosine - second_half * sine, second_half * cosine + first_half * sine], axis=-1)

def rope_tables(positions, head_dim):
    freq_index = jnp.arange(head_dim // 2, dtype=jnp.float32)
    inverse = jnp.exp(freq_index * (-2.0 / head_dim) * math.log(rope_base))
    angles = positions.astype(jnp.float32)[:, None] * inverse[None, :]
    return (jnp.cos(angles), jnp.sin(angles))

def matmul(left, right):
    return jnp.dot(left, right, precision=lax.Precision.HIGHEST)

def doc_positions(segment_row):
    length = segment_row.shape[0]
    earlier = lax.optimization_barrier(jnp.sum((segment_row[None, :] < segment_row[:, None]).astype(jnp.int32), axis=1))
    return jnp.arange(length, dtype=jnp.int32) - earlier

def layer(seq_input, weights, segment_row):
    in_gain, query_gain, key_gain, post_attn_gain, pre_ff_gain, post_ff_gain, w_query, w_key, w_value, w_out, w_gate, w_up, w_down = weights
    length = seq_input.shape[0]
    head_dim = key_gain.shape[0]
    heads = w_query.shape[1] // head_dim
    places = jnp.arange(length, dtype=jnp.int32)
    cosine, sine = rope_tables(doc_positions(segment_row), head_dim)
    normed = low(rms_norm(seq_input, in_gain))
    query_raw = low_back(matmul(normed, w_query)).reshape(length, heads, head_dim)
    key_raw = low_back(matmul(normed, w_key))
    value_rows = low(low_back(matmul(normed, w_value)))
    queries = low(rotate(rms_norm(query_raw, query_gain), cosine[:, None, :], sine[:, None, :]))
    key_rows = low(rotate(rms_norm(key_raw, key_gain), cosine, sine))
    block = math.gcd(length, 512)
    count = length // block

    def one_block(item):
        query_blk, segment_blk, place_blk = item
        scores = low_back(jnp.einsum('thd,kd->htk', query_blk, key_rows, precision=lax.Precision.HIGHEST) * score_scale)
        allowed = (segment_blk[:, None] == segment_row[None, :]) & (place_blk[:, None] >= places[None, :])
        scores = jnp.where(allowed[None], scores, far_below)
        top_score = lax.optimization_barrier(jnp.max(scores, axis=-1, keepdims=True))
        weight = jnp.exp(scores - top_score)
        prob = low(weight / lax.optimization_barrier(jnp.sum(weight, axis=-1, keepdims=True)))
        return jnp.einsum('htk,kd->thd', prob, value_rows, precision=lax.Precision.HIGHEST)
    attended = lax.map(jax.checkpoint(one_block), (queries.reshape(count, block, heads, head_dim), segment_row.reshape(count, block), places.reshape(count, block)))
    attended = low(low_back(attended.reshape(length, heads * head_dim)))
    attn_out = low_back(matmul(attended, w_out))
    middle = seq_input + rms_norm(attn_out, post_attn_gain)
    normed_ff = low(rms_norm(middle, pre_ff_gain))
    gate_pre = low_back(matmul(normed_ff, w_gate))
    up_pre = low_back(matmul(normed_ff, w_up))
    mixed_low = low(jax.nn.gelu(gate_pre, approximate=True) * up_pre)
    branch_out = low_back(matmul(mixed_low, w_down))
    return middle + rms_norm(branch_out, post_ff_gain)

def reference(activations, cotangent, segments, in_gain, query_gain, key_gain, post_attn_gain, pre_ff_gain, post_ff_gain, w_query, w_key, w_value, w_out, w_gate, w_up, w_down):
    weights = tuple((item.astype(jnp.float32) for item in (in_gain, query_gain, key_gain, post_attn_gain, pre_ff_gain, post_ff_gain, w_query, w_key, w_value, w_out, w_gate, w_up, w_down)))
    group = math.gcd(SEQS, max(1, 4096 // LENGTH))
    inputs = activations.astype(jnp.float32).reshape(SEQS // group, group, LENGTH, D)
    upstream = cotangent.astype(jnp.float32).reshape(SEQS // group, group, LENGTH, D)
    seg_groups = segments.reshape(SEQS // group, group, LENGTH)

    def step(totals, item):
        input_grp, upstream_grp, segment_grp = item

        def run(input_in, weights_in):
            return jax.vmap(layer, in_axes=(0, None, 0))(input_in, weights_in, segment_grp)
        result, pull = jax.vjp(run, input_grp, weights)
        grad_input, grad_weights = pull(upstream_grp)
        summed = tuple((total + grad for total, grad in zip(totals, grad_weights)))
        return (summed, (result.astype(jnp.bfloat16), grad_input))
    zeros = tuple((jnp.zeros_like(item) for item in weights))
    totals, (results, grad_inputs) = lax.scan(step, zeros, (inputs, upstream, seg_groups))
    output = results.reshape(SEQS, LENGTH, D)
    input_grad = grad_inputs.reshape(SEQS, LENGTH, D)
    return (output, input_grad, totals[0], totals[1], totals[2], totals[3], totals[4], totals[5], totals[6], totals[7], totals[8], totals[9], totals[10], totals[11], totals[12])
```

```python
import math

import jax
import jax.numpy as jnp
from jax import lax
from jax.sharding import PartitionSpec as P

norm_eps = 1e-06
rope_base = 1000000.0
score_scale = 0.0625
far_below = -1e30
f32 = jnp.float32
bf16 = jnp.bfloat16
pack_rows = 16


def rms_norm(values, gain):
    factor = lax.rsqrt(jnp.mean(values * values, axis=-1, keepdims=True) + norm_eps)
    return values * factor * (1.0 + gain)


def rotate(values, cosine, sine):
    half_dim = values.shape[-1] // 2
    first_half = values[..., :half_dim]
    second_half = values[..., half_dim:]
    return jnp.concatenate(
        [first_half * cosine - second_half * sine, second_half * cosine + first_half * sine],
        axis=-1,
    )


def rope_tables(positions, head_dim):
    freq_index = jnp.arange(head_dim // 2, dtype=f32)
    inverse = jnp.exp(freq_index * (-2.0 / head_dim) * math.log(rope_base))
    angles = positions.astype(f32)[:, None] * inverse[None, :]
    return (jnp.cos(angles), jnp.sin(angles))


def gated_unit(gate_pre, up_pre):
    return jax.nn.gelu(gate_pre, approximate=True) * up_pre


def contract(left, right, left_dim, right_dim, kind=f32):
    return lax.dot_general(
        left, right, (((left_dim,), (right_dim,)), ((), ())), preferred_element_type=kind
    )


def from_ahead(block, step):
    size = lax.axis_size("ctx")
    return lax.ppermute(block, "ctx", [(i, (i - step) % size) for i in range(size)])


def to_ahead(block, step):
    size = lax.axis_size("ctx")
    return lax.ppermute(block, "ctx", [(i, (i + step) % size) for i in range(size)])


def gather_ahead(block):
    size = lax.axis_size("ctx")
    return jnp.concatenate([block] + [from_ahead(block, s) for s in range(1, size)], axis=0)


def sum_ahead(terms):
    arrived = [to_ahead(terms[s].astype(bf16), s) for s in range(1, len(terms))]
    total = terms[0].astype(f32)
    for item in arrived:
        total = total + item.astype(f32)
    return total


def swap_ctx(pieces):
    size = pieces.shape[0]
    me = lax.axis_index("ctx")
    result = jnp.zeros_like(pieces)
    own = lax.dynamic_index_in_dim(pieces, me, 0, keepdims=True)
    result = lax.dynamic_update_slice_in_dim(result, own, me, 0)
    for s in range(1, size):
        item = lax.dynamic_index_in_dim(pieces, (me + s) % size, 0, keepdims=True)
        item = to_ahead(item, s)
        result = lax.dynamic_update_slice_in_dim(result, item, (me - s) % size, 0)
    return result


def owner_pairs(outer, inner):
    return [(d, (d % outer) * inner + d // outer) for d in range(outer * inner)]


def local(
    activations,
    cotangent,
    segments,
    in_gain,
    query_gain,
    key_gain,
    post_attn_gain,
    pre_ff_gain,
    post_ff_gain,
    w_query,
    w_key,
    w_value,
    w_out,
    w_gate,
    w_up,
    w_down,
):
    outer = lax.axis_size("dp")
    inner = lax.axis_size("ctx")
    owners = outer * inner
    me = lax.axis_index("ctx")
    rows = w_query.shape[0]
    model = rows * owners
    qkv_cols = w_query.shape[1] + w_key.shape[1] + w_value.shape[1]
    query_cols = w_query.shape[1]
    head_dim = w_key.shape[1]
    heads = query_cols // head_dim
    out_rows = w_out.shape[0] * w_out.shape[1] // qkv_cols

    gains = (in_gain, query_gain, key_gain, post_attn_gain, pre_ff_gain, post_ff_gain)
    gain_row = jnp.concatenate(gains)
    gain_row = jnp.pad(gain_row, (0, qkv_cols - gain_row.shape[0]))[None]
    packed = jnp.concatenate(
        [
            jnp.concatenate([w_query, w_key, w_value], axis=1),
            w_out.reshape(out_rows, qkv_cols),
            gain_row,
        ],
        axis=0,
    )
    attn_all = lax.all_gather(packed, ("dp", "ctx"), axis=0, tiled=True)
    by_owner = attn_all.reshape(owners, pack_rows, qkv_cols)
    full_out = by_owner[:, rows : rows + out_rows, :].reshape(query_cols, model)
    gain_all = by_owner[:, pack_rows - 1, :128].astype(f32)
    full_gains = []
    first = 0
    for item in gains:
        size = item.shape[0]
        full_gains.append(gain_all[:, first : first + size].reshape(size * owners))
        first += size
    gain_in, gain_query, gain_key, gain_post_attn, gain_pre, gain_post = full_gains

    part = w_gate.shape[1] // inner
    both = jnp.concatenate(
        [w_gate.reshape(rows, inner, part), w_up.reshape(rows, inner, part)], axis=2
    ).transpose(1, 0, 2)
    both = swap_ctx(both).reshape(inner * rows, 2 * part)
    down_part = lax.ppermute(w_down, ("dp", "ctx"), owner_pairs(outer, inner))
    down_rows = w_down.shape[0] // 3
    ffn_packed = jnp.concatenate(
        [
            both,
            jnp.concatenate([down_part[i * down_rows : (i + 1) * down_rows] for i in range(3)], axis=1),
        ],
        axis=0,
    )
    ffn_all = lax.all_gather(ffn_packed, "dp", axis=0, tiled=False)
    full_both = ffn_all[:, : inner * rows, :].reshape(model, 2 * part)
    full_down = (
        ffn_all[:, inner * rows :, :]
        .reshape(outer, down_rows, 3, model)
        .transpose(0, 2, 1, 3)
        .reshape(part, model)
    )

    inputs = activations[0].astype(f32)
    segment_all = segments[0]
    tok_count = inputs.shape[0]
    first_place = me * tok_count
    place_rows = first_place + jnp.arange(tok_count, dtype=jnp.int32)
    segment_rows = lax.dynamic_slice_in_dim(segment_all, first_place, tok_count)
    earlier = jnp.sum((segment_all[None, :] < segment_rows[:, None]).astype(jnp.int32), axis=1)
    cosine, sine = rope_tables(place_rows - earlier, head_dim)
    length = segment_all.shape[0]
    key_places = (first_place + jnp.arange(length, dtype=jnp.int32)) % length
    key_segments = jnp.take(segment_all, key_places)
    allowed = (segment_rows[:, None] == key_segments[None, :]) & (
        place_rows[:, None] >= key_places[None, :]
    )
    allowed = jnp.tile(allowed, (heads, 1))

    model_index = jnp.arange(model, dtype=jnp.int32)
    padded_index = model_index // rows * pack_rows + model_index % rows
    spread = (
        padded_index[:, None] == jnp.arange(owners * pack_rows, dtype=jnp.int32)[None, :]
    ).astype(bf16)

    normed, in_pull = jax.vjp(rms_norm, inputs, gain_in)
    normed_wide = contract(normed.astype(bf16), spread, 1, 0, bf16)
    qkv = contract(normed_wide, attn_all, 1, 0)
    query_raw = qkv[:, :query_cols].reshape(tok_count, heads, head_dim)
    key_raw = qkv[:, query_cols : query_cols + head_dim]
    value_low = qkv[:, query_cols + head_dim :].astype(bf16)

    def prepare(query_in, key_in, query_scale, key_scale):
        rotated_query = rotate(
            rms_norm(query_in, query_scale), cosine[:, None, :], sine[:, None, :]
        )
        rotated_key = rotate(rms_norm(key_in, key_scale), cosine, sine)
        return (rotated_query, rotated_key)

    (queries, key_rows), prepare_pull = jax.vjp(prepare, query_raw, key_raw, gain_query, gain_key)
    query_low = queries.astype(bf16).transpose(1, 0, 2).reshape(heads * tok_count, head_dim)
    key_value = gather_ahead(jnp.concatenate([key_rows.astype(bf16), value_low], axis=1))
    key_all = key_value[:, :head_dim]
    value_all = key_value[:, head_dim:]

    scores = contract(query_low, key_all, 1, 1) * score_scale
    scores = jnp.where(allowed, scores, far_below)
    top_score = jnp.max(scores, axis=-1, keepdims=True)
    weight = jnp.exp(scores - top_score)
    prob = weight / jnp.sum(weight, axis=-1, keepdims=True)
    prob_low = prob.astype(bf16)
    attended = contract(prob_low, value_all, 1, 0).astype(bf16)
    attended_low = attended.reshape(heads, tok_count, head_dim).transpose(1, 0, 2)
    attended_low = attended_low.reshape(tok_count, query_cols)
    attn_out = contract(attended_low, full_out, 1, 0)
    post_attn, post_attn_pull = jax.vjp(rms_norm, attn_out, gain_post_attn)
    middle = inputs + post_attn
    normed_ff, pre_pull = jax.vjp(rms_norm, middle, gain_pre)
    normed_all = gather_ahead(normed_ff.astype(bf16))

    gate_up = contract(normed_all, full_both, 1, 0)
    mixed, gated_pull = jax.vjp(gated_unit, gate_up[:, :part], gate_up[:, part:])
    mixed_low = mixed.astype(bf16)
    branch_term = contract(mixed_low, full_down, 1, 0)
    branch_out = sum_ahead(
        [branch_term[s * tok_count : (s + 1) * tok_count] for s in range(inner)]
    )
    post_ff, post_pull = jax.vjp(rms_norm, branch_out, gain_post)
    output = (middle + post_ff).astype(bf16)

    grad_output = cotangent[0].astype(f32)
    grad_branch, grad_post_ff = post_pull(grad_output)
    grad_branch_all = gather_ahead(grad_branch.astype(bf16))
    down_term = contract(mixed_low, grad_branch_all, 0, 0, bf16)
    grad_mixed = contract(grad_branch_all, full_down, 1, 1)
    grad_gate, grad_up = gated_pull(grad_mixed)
    grad_both = jnp.concatenate([grad_gate.astype(bf16), grad_up.astype(bf16)], axis=1)
    both_term = contract(normed_all, grad_both, 0, 0, bf16)
    grad_normed_term = contract(grad_both, full_both, 1, 1)
    ffn_terms = jnp.concatenate(
        [
            both_term.reshape(outer, inner * rows, 2 * part),
            down_term.reshape(outer, 3, down_rows, model)
            .transpose(0, 2, 1, 3)
            .reshape(outer, down_rows, 2 * part),
            jnp.zeros((outer, -(inner * rows + down_rows) % 64, 2 * part), bf16),
        ],
        axis=1,
    )
    ffn_sum = lax.psum_scatter(
        ffn_terms.reshape(-1, 2 * part), "dp", scatter_dimension=0, tiled=True
    )
    both_grad = swap_ctx(ffn_sum[: inner * rows].reshape(inner, rows, 2 * part))
    both_grad = both_grad.astype(f32).transpose(1, 0, 2)
    gate_grad = both_grad[:, :, :part].reshape(rows, inner * part)
    up_grad = both_grad[:, :, part:].reshape(rows, inner * part)
    down_grad = jnp.concatenate(
        [
            ffn_sum[inner * rows : inner * rows + down_rows, i * model : (i + 1) * model]
            for i in range(3)
        ], axis=0
    )
    down_grad = lax.ppermute(
        down_grad, ("dp", "ctx"), [(b, a) for a, b in owner_pairs(outer, inner)]
    ).astype(f32)

    grad_normed_ff = sum_ahead(
        [grad_normed_term[s * tok_count : (s + 1) * tok_count] for s in range(inner)]
    )
    grad_middle_add, grad_pre_ff = pre_pull(grad_normed_ff)
    grad_middle = grad_output + grad_middle_add
    grad_attn, grad_post_attn = post_attn_pull(grad_middle)
    grad_attn_low = grad_attn.astype(bf16)
    out_term = contract(attended_low, grad_attn_low, 0, 0, bf16)
    grad_attended = contract(grad_attn_low, full_out, 1, 1, bf16)
    grad_attended = grad_attended.reshape(tok_count, heads, head_dim).transpose(1, 0, 2)
    grad_attended = grad_attended.reshape(heads * tok_count, head_dim)

    grad_prob = contract(grad_attended, value_all, 1, 1)
    shift_term = jnp.sum(prob * grad_prob, axis=-1, keepdims=True)
    grad_scores = (prob * (grad_prob - shift_term)).astype(bf16)
    grad_query = contract(grad_scores, key_all, 1, 0) * score_scale
    grad_key = contract(grad_scores, query_low, 0, 0) * score_scale
    grad_value = contract(prob_low, grad_attended, 0, 0)
    grad_key_value = jnp.concatenate([grad_key, grad_value], axis=1)
    grad_key_value = sum_ahead(
        [grad_key_value[s * tok_count : (s + 1) * tok_count] for s in range(inner)]
    )
    grad_queries = grad_query.reshape(heads, tok_count, head_dim).transpose(1, 0, 2)
    grad_query_raw, grad_key_raw, grad_query_gain, grad_key_gain = prepare_pull(
        (grad_queries, grad_key_value[:, :head_dim])
    )
    grad_qkv = jnp.concatenate(
        [
            grad_query_raw.reshape(tok_count, query_cols),
            grad_key_raw,
            grad_key_value[:, head_dim:],
        ],
        axis=1,
    ).astype(bf16)
    qkv_term = contract(normed_wide, grad_qkv, 0, 0, bf16)
    grad_normed_wide = contract(grad_qkv, attn_all, 1, 1, bf16)
    grad_normed = contract(grad_normed_wide, spread, 1, 1)
    grad_input_add, grad_in_gain = in_pull(grad_normed)
    input_grad = grad_middle + grad_input_add

    grad_gains = (
        grad_in_gain,
        grad_query_gain,
        grad_key_gain,
        grad_post_attn,
        grad_pre_ff,
        grad_post_ff,
    )
    gain_terms = jnp.concatenate([item.reshape(owners, -1) for item in grad_gains], axis=1)
    gain_terms = jnp.pad(gain_terms, ((0, 0), (0, qkv_cols - gain_terms.shape[1])))
    attn_terms = jnp.concatenate(
        [
            qkv_term.reshape(owners, pack_rows, qkv_cols)[:, :rows],
            out_term.reshape(owners, out_rows, qkv_cols),
            gain_terms[:, None].astype(bf16),
        ],
        axis=1,
    ).reshape(outer, inner, pack_rows, qkv_cols)
    attn_sum = lax.psum_scatter(attn_terms, "dp", scatter_dimension=0, tiled=False)
    attn_swapped = swap_ctx(attn_sum).astype(f32)
    attn_grad = jnp.sum(attn_swapped, axis=0)
    gain_grads = []
    first = 0
    for item in gains:
        size = item.shape[0]
        gain_grads.append(attn_grad[pack_rows - 1, first : first + size])
        first += size
    return (
        output[None],
        input_grad[None],
        *gain_grads,
        attn_grad[:rows, :query_cols],
        attn_grad[:rows, query_cols : query_cols + head_dim],
        attn_grad[:rows, query_cols + head_dim :],
        attn_grad[rows : rows + out_rows].reshape(w_out.shape),
        gate_grad,
        up_grad,
        down_grad,
    )


def solution(mesh):
    shard = P(("dp", "ctx"))
    matrix = P(("dp", "ctx"), None)
    tokens = P("dp", "ctx", None)
    return jax.shard_map(
        local,
        mesh=mesh,
        in_specs=(tokens, tokens, P("dp", None)) + (shard,) * 6 + (matrix,) * 7,
        out_specs=(tokens, tokens) + (shard,) * 6 + (matrix,) * 7,
        check_vma=False,
    )
```

```python
import math

import jax
import jax.numpy as jnp
from jax import lax
from jax.sharding import Mesh
from jax.sharding import PartitionSpec as P

norm_eps = 1e-06
rope_base = 1000000.0
score_scale = 0.0625
far_below = -1e30
f32 = jnp.float32
bf16 = jnp.bfloat16


def rms_norm(values, gain):
    factor = lax.rsqrt(jnp.mean(values * values, axis=-1, keepdims=True) + norm_eps)
    return values * factor * (1.0 + gain)


def rotate(values, cosine, sine):
    half_dim = values.shape[-1] // 2
    first_half = values[..., :half_dim]
    second_half = values[..., half_dim:]
    return jnp.concatenate(
        [first_half * cosine - second_half * sine, second_half * cosine + first_half * sine],
        axis=-1,
    )


def rope_tables(positions, head_dim):
    freq_index = jnp.arange(head_dim // 2, dtype=f32)
    inverse = jnp.exp(freq_index * (-2.0 / head_dim) * math.log(rope_base))
    angles = positions.astype(f32)[:, None] * inverse[None, :]
    return (jnp.cos(angles), jnp.sin(angles))


def gated_unit(gate_pre, up_pre):
    return jax.nn.gelu(gate_pre, approximate=True) * up_pre


def contract(left, right, left_dim, right_dim, kind=f32):
    return lax.dot_general(
        left, right, (((left_dim,), (right_dim,)), ((), ())), preferred_element_type=kind
    )


def from_ahead(block, step, axis="y"):
    size = lax.axis_size(axis)
    return lax.ppermute(block, axis, [(i, (i - step) % size) for i in range(size)])


def to_ahead(block, step, axis="y"):
    size = lax.axis_size(axis)
    return lax.ppermute(block, axis, [(i, (i + step) % size) for i in range(size)])


def gather_ahead(block, axis="y"):
    size = lax.axis_size(axis)
    return jnp.concatenate([block] + [from_ahead(block, s, axis) for s in range(1, size)], axis=0)


def sum_ahead(terms, axis="y"):
    arrived = [to_ahead(terms[s].astype(bf16), s, axis) for s in range(1, len(terms))]
    total = terms[0].astype(f32)
    for item in arrived:
        total = total + item.astype(f32)
    return total


def swap(pieces, axis):
    size = lax.axis_size(axis)
    me = lax.axis_index(axis)
    arrived = [lax.dynamic_index_in_dim(pieces, me, 0, keepdims=False)]
    for s in range(1, size):
        item = lax.dynamic_index_in_dim(pieces, (me + s) % size, 0, keepdims=False)
        arrived.append(to_ahead(item, s, axis))
    return by_sender(arrived, axis)


def by_sender(arrived, axis):
    size = lax.axis_size(axis)
    me = lax.axis_index(axis)
    result = []
    for c in range(size):
        item = arrived[0]
        for s in range(1, size):
            item = jnp.where((me - c) % size == s, arrived[s], item)
        result.append(item)
    return jnp.stack(result)


def gather_blocks(block, axis):
    size = lax.axis_size(axis)
    return by_sender([block] + [to_ahead(block, s, axis) for s in range(1, size)], axis)


def gather_team(block):
    return gather_ahead(gather_ahead(block, "y"), "core")


def sum_team(term, tokens):
    half = term.shape[0] // 2
    term = sum_ahead([term[:half], term[half:]], "core")
    return sum_ahead([term[i : i + tokens] for i in range(0, half, tokens)], "y")


def down_routes(teams, members):
    here, before = [], []
    for member in range(members):
        for block in range(teams):
            owner = member * teams + block
            here.append((owner, block * members + member))
            if block > 0:
                before.append((owner, (block - 1) * members + member))
    return here, before


def local(
    activations,
    cotangent,
    segments,
    in_gain,
    query_gain,
    key_gain,
    post_attn_gain,
    pre_ff_gain,
    post_ff_gain,
    w_query,
    w_key,
    w_value,
    w_out,
    w_gate,
    w_up,
    w_down,
):
    all_axes = ("x", "z", "core", "y")
    teams = lax.axis_size("x") * lax.axis_size("z")
    inner = lax.axis_size("y")
    cores = lax.axis_size("core")
    members = inner * cores
    me = lax.axis_index("y")
    team = lax.axis_index("x") * lax.axis_size("z") + lax.axis_index("z")
    flat = team * members + lax.axis_index("core") * inner + me
    rows = w_query.shape[0]
    model = w_down.shape[1]
    query_cols = w_query.shape[1]
    head_dim = w_key.shape[1]
    heads = query_cols // head_dim
    qkv_cols = query_cols + 2 * head_dim
    out_rows = w_out.shape[0]
    team_rows = members * rows
    part = w_gate.shape[1] // members
    wide = -(-part // 128) * 128
    down_rows = w_down.shape[0]
    down_wide = wide // teams
    down_shift = down_wide - down_rows

    def columns(weight):
        pieces = weight.reshape(rows, members, part)
        return jnp.pad(pieces, ((0, 0), (0, 0), (0, wide - part)))

    both = jnp.concatenate([columns(w_gate), columns(w_up)], axis=2).transpose(1, 0, 2)
    both = both.reshape(cores, inner, rows, 2 * wide)
    gains = (in_gain, query_gain, key_gain, post_attn_gain, pre_ff_gain, post_ff_gain)
    gain_row = jnp.concatenate(gains)
    gain_row = jnp.pad(gain_row, (0, model - gain_row.shape[0]))[None]
    attn_rows = jnp.concatenate(
        [w_query, w_key, w_value, jnp.concatenate([w_out, gain_row], axis=0)], axis=1
    )
    first_message = jnp.concatenate(
        [
            both.transpose(1, 2, 0, 3).reshape(inner, rows, cores * 2 * wide),
            jnp.broadcast_to(attn_rows[None], (inner,) + attn_rows.shape),
        ],
        axis=2,
    )
    by_y = swap(first_message, "y")
    attn_y = by_y[:, :, cores * 2 * wide :]
    second_message = jnp.stack(
        [
            jnp.concatenate([by_y[:, :, c * 2 * wide : (c + 1) * 2 * wide], attn_y], axis=2)
            for c in range(cores)
        ]
    )
    by_member = swap(second_message, "core").reshape(members, rows, -1)
    out_part = by_member[:, :, 2 * wide + qkv_cols :]
    here, before = down_routes(teams, members)
    down_two = jnp.concatenate(
        [lax.ppermute(w_down, all_axes, here), lax.ppermute(w_down, all_axes, before)], axis=0
    )
    down_part = lax.dynamic_slice_in_dim(down_two, down_shift * team, down_wide, 0)
    shard = jnp.concatenate(
        [
            by_member[:, :, : 2 * wide].reshape(team_rows, 2 * wide),
            jnp.pad(down_part, ((0, team_rows - down_wide), (0, 0))),
            by_member[:, :, 2 * wide : 2 * wide + qkv_cols].reshape(team_rows, qkv_cols),
            jnp.concatenate(
                [out_part[:, :out_rows].reshape(members * out_rows, model), out_part[:, out_rows]],
                axis=0,
            ),
        ],
        axis=1,
    )
    full = lax.all_gather(shard, ("x", "z"), axis=0, tiled=True)
    first = 2 * wide
    full_both = full[:, :first]
    by_team = full.reshape(teams, team_rows, -1)
    full_down = by_team[:, :down_wide, first : first + model].reshape(wide, model)
    first += model
    full_qkv = full[:, first : first + qkv_cols]
    first += qkv_cols
    full_out = by_team[:, : members * out_rows, first : first + model].reshape(query_cols, model)
    gain_all = by_team[:, members * out_rows :, first : first + 128].astype(f32)
    full_gains = []
    first = 0
    for item in gains:
        size = item.shape[0]
        full_gains.append(gain_all[:, :, first : first + size].reshape(-1))
        first += size
    gain_in, gain_query, gain_key, gain_post_attn, gain_pre, gain_post = full_gains

    inputs = activations[0].astype(f32)
    segment_all = segments[0]
    tok_count = inputs.shape[0]
    first_place = me * tok_count
    place_rows = first_place + jnp.arange(tok_count, dtype=jnp.int32)
    segment_rows = lax.dynamic_slice_in_dim(segment_all, first_place, tok_count)
    earlier = jnp.sum((segment_all[None, :] < segment_rows[:, None]).astype(jnp.int32), axis=1)
    cosine, sine = rope_tables(place_rows - earlier, head_dim)
    length = segment_all.shape[0]
    key_places = (first_place + jnp.arange(length, dtype=jnp.int32)) % length
    key_segments = jnp.take(segment_all, key_places)
    allowed = (segment_rows[:, None] == key_segments[None, :]) & (
        place_rows[:, None] >= key_places[None, :]
    )
    allowed = jnp.tile(allowed, (heads, 1))

    normed, in_pull = jax.vjp(rms_norm, inputs, gain_in)
    normed_low = normed.astype(bf16)
    qkv = contract(normed_low, full_qkv, 1, 0)
    query_raw = qkv[:, :query_cols].reshape(tok_count, heads, head_dim)
    key_raw = qkv[:, query_cols : query_cols + head_dim]
    value_low = qkv[:, query_cols + head_dim :].astype(bf16)

    def prepare(query_in, key_in, query_scale, key_scale):
        rotated_query = rotate(
            rms_norm(query_in, query_scale), cosine[:, None, :], sine[:, None, :]
        )
        rotated_key = rotate(rms_norm(key_in, key_scale), cosine, sine)
        return (rotated_query, rotated_key)

    (queries, key_rows), prepare_pull = jax.vjp(prepare, query_raw, key_raw, gain_query, gain_key)
    query_low = queries.astype(bf16).transpose(1, 0, 2).reshape(heads * tok_count, head_dim)
    key_value = gather_ahead(jnp.concatenate([key_rows.astype(bf16), value_low], axis=1))
    key_all = key_value[:, :head_dim]
    value_all = key_value[:, head_dim:]

    scores = contract(query_low, key_all, 1, 1) * score_scale
    scores = jnp.where(allowed, scores, far_below)
    top_score = jnp.max(scores, axis=-1, keepdims=True)
    weight = jnp.exp(scores - top_score)
    prob = weight / jnp.sum(weight, axis=-1, keepdims=True)
    prob_low = prob.astype(bf16)
    attended = contract(prob_low, value_all, 1, 0).astype(bf16)
    attended_low = attended.reshape(heads, tok_count, head_dim).transpose(1, 0, 2)
    attended_low = attended_low.reshape(tok_count, query_cols)
    attn_out = contract(attended_low, full_out, 1, 0)
    post_attn, post_attn_pull = jax.vjp(rms_norm, attn_out, gain_post_attn)
    middle = inputs + post_attn
    normed_ff, pre_pull = jax.vjp(rms_norm, middle, gain_pre)
    normed_all = gather_team(normed_ff.astype(bf16))

    gate_up = contract(normed_all, full_both, 1, 0)
    mixed, gated_pull = jax.vjp(gated_unit, gate_up[:, :wide], gate_up[:, wide:])
    mixed_low = mixed.astype(bf16)
    branch_term = contract(mixed_low, full_down, 1, 0)
    branch_out = sum_team(branch_term, tok_count)
    post_ff, post_pull = jax.vjp(rms_norm, branch_out, gain_post)
    output = (middle + post_ff).astype(bf16)

    grad_output = cotangent[0].astype(f32)
    grad_branch, grad_post_ff = post_pull(grad_output)
    grad_branch_all = gather_team(grad_branch.astype(bf16))
    down_term = contract(mixed_low, grad_branch_all, 0, 0, bf16)
    grad_mixed = contract(grad_branch_all, full_down, 1, 1)
    grad_gate, grad_up = gated_pull(grad_mixed)
    grad_both = jnp.concatenate([grad_gate.astype(bf16), grad_up.astype(bf16)], axis=1)
    both_term = contract(normed_all, grad_both, 0, 0, bf16)
    grad_normed_term = contract(grad_both, full_both, 1, 1)
    ffn_terms = jnp.concatenate(
        [
            both_term.reshape(teams, team_rows, 2 * wide),
            jnp.pad(
                down_term.reshape(teams, down_wide, model),
                ((0, 0), (0, team_rows - down_wide), (0, 0)),
            ),
        ],
        axis=2,
    ).reshape(teams * team_rows, -1)
    ffn_terms, grad_normed_term = lax.optimization_barrier((ffn_terms, grad_normed_term))
    ffn_sum = lax.psum_scatter(ffn_terms.reshape(teams, team_rows, -1), ("x", "z"), scatter_dimension=0, tiled=True)[0]
    both_grad = ffn_sum[:, : 2 * wide].reshape(cores, inner, rows, 2 * wide).transpose(1, 0, 2, 3)
    both_grad = swap(both_grad, "y").transpose(1, 0, 2, 3)
    both_grad = swap(both_grad, "core").reshape(members, rows, 2 * wide).astype(f32)
    both_grad = both_grad.transpose(1, 0, 2)
    gate_grad = both_grad[:, :, :part].reshape(rows, members * part)
    up_grad = both_grad[:, :, wide : wide + part].reshape(rows, members * part)
    down_sum = ffn_sum[:down_wide, 2 * wide :]
    down_two = jnp.concatenate(
        [
            lax.ppermute(down_sum, all_axes, [(b, a) for a, b in before]),
            lax.ppermute(down_sum, all_axes, [(b, a) for a, b in here]),
        ],
        axis=0,
    )
    down_grad = lax.dynamic_slice_in_dim(
        down_two, down_wide - down_shift * (flat % teams), down_rows, 0
    ).astype(f32)

    grad_normed_ff = sum_team(grad_normed_term, tok_count)
    grad_middle_add, grad_pre_ff = pre_pull(grad_normed_ff)
    grad_middle = grad_output + grad_middle_add
    grad_attn, grad_post_attn = post_attn_pull(grad_middle)
    grad_attn_low = grad_attn.astype(bf16)
    out_term = contract(attended_low, grad_attn_low, 0, 0, bf16)
    grad_attended = contract(grad_attn_low, full_out, 1, 1, bf16)
    grad_attended = grad_attended.reshape(tok_count, heads, head_dim).transpose(1, 0, 2)
    grad_attended = grad_attended.reshape(heads * tok_count, head_dim)

    grad_prob = contract(grad_attended, value_all, 1, 1)
    shift_term = jnp.sum(prob * grad_prob, axis=-1, keepdims=True)
    grad_scores = (prob * (grad_prob - shift_term)).astype(bf16)
    grad_query = contract(grad_scores, key_all, 1, 0) * score_scale
    grad_key = contract(grad_scores, query_low, 0, 0) * score_scale
    grad_value = contract(prob_low, grad_attended, 0, 0)
    grad_key_value = jnp.concatenate([grad_key, grad_value], axis=1)
    grad_key_value = sum_ahead(
        [grad_key_value[s * tok_count : (s + 1) * tok_count] for s in range(inner)]
    )
    grad_queries = grad_query.reshape(heads, tok_count, head_dim).transpose(1, 0, 2)
    grad_query_raw, grad_key_raw, grad_query_gain, grad_key_gain = prepare_pull(
        (grad_queries, grad_key_value[:, :head_dim])
    )
    grad_qkv = jnp.concatenate(
        [
            grad_query_raw.reshape(tok_count, query_cols),
            grad_key_raw,
            grad_key_value[:, head_dim:],
        ],
        axis=1,
    ).astype(bf16)
    qkv_term = contract(normed_low, grad_qkv, 0, 0, bf16)
    grad_normed = contract(grad_qkv, full_qkv, 1, 1)
    grad_input_add, grad_in_gain = in_pull(grad_normed)
    input_grad = grad_middle + grad_input_add

    grad_gains = (
        grad_in_gain,
        grad_query_gain,
        grad_key_gain,
        grad_post_attn,
        grad_pre_ff,
        grad_post_ff,
    )
    gain_terms = jnp.concatenate(
        [item.reshape(teams, members, -1) for item in grad_gains], axis=2
    ).astype(bf16)
    filling = jnp.broadcast_to(ffn_sum[0, 0], gain_terms.shape[:2] + (model - gain_terms.shape[2],))
    gain_terms = jnp.concatenate([gain_terms, filling], axis=2)
    attn_terms = jnp.concatenate(
        [
            qkv_term.reshape(teams, team_rows, qkv_cols),
            jnp.concatenate(
                [out_term.reshape(teams, members * out_rows, model), gain_terms], axis=1
            ),
        ],
        axis=2,
    ).reshape(teams * team_rows, -1)
    attn_sum = lax.psum_scatter(attn_terms.reshape(teams, team_rows, -1), ("x", "z"), scatter_dimension=0, tiled=True)[0]
    attn_sum = jnp.concatenate(
        [
            attn_sum[:, :qkv_cols].reshape(members, rows, qkv_cols),
            jnp.concatenate(
                [
                    attn_sum[: members * out_rows, qkv_cols:].reshape(members, out_rows, model),
                    attn_sum[members * out_rows :, qkv_cols:][:, None],
                ],
                axis=1,
            ),
        ],
        axis=2,
    ).reshape(cores, inner, rows, qkv_cols + model)
    attn_sum = jnp.sum(swap(attn_sum.transpose(1, 0, 2, 3), "y").astype(f32), axis=0)
    attn_grad = jnp.sum(swap(attn_sum.astype(bf16), "core").astype(f32), axis=0)
    gain_grads = []
    first = qkv_cols
    for item in gains:
        size = item.shape[0]
        gain_grads.append(attn_grad[rows - 1, first : first + size])
        first += size
    return (
        output[None],
        input_grad[None],
        *gain_grads,
        attn_grad[:, :query_cols],
        attn_grad[:, query_cols : query_cols + head_dim],
        attn_grad[:, query_cols + head_dim : qkv_cols],
        attn_grad[:out_rows, qkv_cols:],
        gate_grad,
        up_grad,
        down_grad,
    )


def solution(mesh):
    fine = Mesh(mesh.devices.reshape(4, 4, 2, 4), ("x", "z", "core", "y"))
    all_axes = ("x", "z", "core", "y")
    shard = P(all_axes)
    matrix = P(all_axes, None)
    tokens = P(("x", "z", "core"), "y", None)
    return jax.shard_map(
        local,
        mesh=fine,
        in_specs=(tokens, tokens, P(("x", "z", "core"), None)) + (shard,) * 6 + (matrix,) * 7,
        out_specs=(tokens, tokens) + (shard,) * 6 + (matrix,) * 7,
        check_vma=False,
    )
```

```python
import math

import jax
import jax.numpy as jnp
from jax import lax
from jax.sharding import Mesh
from jax.sharding import PartitionSpec as P

norm_eps = 1e-06
rope_base = 1000000.0
score_scale = 0.0625
far_below = -1e30
f32 = jnp.float32
bf16 = jnp.bfloat16


def rms_norm(values, gain):
    factor = lax.rsqrt(jnp.mean(values * values, axis=-1, keepdims=True) + norm_eps)
    return values * factor * (1.0 + gain)


def rotate(values, cosine, sine):
    half_dim = values.shape[-1] // 2
    first_half = values[..., :half_dim]
    second_half = values[..., half_dim:]
    return jnp.concatenate(
        [first_half * cosine - second_half * sine, second_half * cosine + first_half * sine],
        axis=-1,
    )


def rope_tables(positions, head_dim):
    freq_index = jnp.arange(head_dim // 2, dtype=f32)
    inverse = jnp.exp(freq_index * (-2.0 / head_dim) * math.log(rope_base))
    angles = positions.astype(f32)[:, None] * inverse[None, :]
    return (jnp.cos(angles), jnp.sin(angles))


def gated_unit(gate_pre, up_pre):
    return jax.nn.gelu(gate_pre, approximate=True) * up_pre


def contract(left, right, left_dim, right_dim, kind=f32):
    return lax.dot_general(
        left, right, (((left_dim,), (right_dim,)), ((), ())), preferred_element_type=kind
    )


def from_ahead(block, step, axis="y"):
    size = lax.axis_size(axis)
    return lax.ppermute(block, axis, [(i, (i - step) % size) for i in range(size)])


def to_ahead(block, step, axis="y"):
    size = lax.axis_size(axis)
    return lax.ppermute(block, axis, [(i, (i + step) % size) for i in range(size)])


def gather_ahead(block, axis="y"):
    size = lax.axis_size(axis)
    return jnp.concatenate([block] + [from_ahead(block, s, axis) for s in range(1, size)], axis=0)


def sum_ahead(terms, axis="y"):
    arrived = [to_ahead(terms[s].astype(bf16), s, axis) for s in range(1, len(terms))]
    total = terms[0].astype(f32)
    for item in arrived:
        total = total + item.astype(f32)
    return total


def swap(pieces, axis):
    size = lax.axis_size(axis)
    me = lax.axis_index(axis)
    arrived = [lax.dynamic_index_in_dim(pieces, me, 0, keepdims=False)]
    for s in range(1, size):
        item = lax.dynamic_index_in_dim(pieces, (me + s) % size, 0, keepdims=False)
        arrived.append(to_ahead(item, s, axis))
    return by_sender(arrived, axis)


def by_sender(arrived, axis):
    size = lax.axis_size(axis)
    me = lax.axis_index(axis)
    result = []
    for c in range(size):
        item = arrived[0]
        for s in range(1, size):
            item = jnp.where((me - c) % size == s, arrived[s], item)
        result.append(item)
    return jnp.stack(result)


def reduce_axis(terms, axis, dim):
    size = lax.axis_size(axis)
    me = lax.axis_index(axis)
    total = lax.dynamic_index_in_dim(terms, me, dim, keepdims=False).astype(f32)
    arrived = [
        to_ahead(lax.dynamic_index_in_dim(terms, (me + s) % size, dim, keepdims=False), s, axis)
        for s in range(1, size)
    ]
    for item in arrived:
        total = total + item.astype(f32)
    return total.astype(bf16)


def gather_blocks(block, axis):
    size = lax.axis_size(axis)
    return by_sender([block] + [to_ahead(block, s, axis) for s in range(1, size)], axis)


def gather_team(block):
    return gather_ahead(gather_ahead(block, "y"), "core")


def sum_team(term, tokens):
    half = term.shape[0] // 2
    term = sum_ahead([term[:half], term[half:]], "core")
    return sum_ahead([term[i : i + tokens] for i in range(0, half, tokens)], "y")


def down_routes(teams, members):
    here, before = [], []
    for member in range(members):
        for block in range(teams):
            owner = member * teams + block
            here.append((owner, block * members + member))
            if block > 0:
                before.append((owner, (block - 1) * members + member))
    return here, before


def local(
    activations,
    cotangent,
    segments,
    in_gain,
    query_gain,
    key_gain,
    post_attn_gain,
    pre_ff_gain,
    post_ff_gain,
    w_query,
    w_key,
    w_value,
    w_out,
    w_gate,
    w_up,
    w_down,
):
    all_axes = ("x", "z", "core", "y")
    teams = lax.axis_size("x") * lax.axis_size("z")
    inner = lax.axis_size("y")
    cores = lax.axis_size("core")
    members = inner * cores
    me = lax.axis_index("y")
    team = lax.axis_index("x") * lax.axis_size("z") + lax.axis_index("z")
    flat = team * members + lax.axis_index("core") * inner + me
    rows = w_query.shape[0]
    model = w_down.shape[1]
    query_cols = w_query.shape[1]
    head_dim = w_key.shape[1]
    heads = query_cols // head_dim
    qkv_cols = query_cols + 2 * head_dim
    out_rows = w_out.shape[0]
    team_rows = members * rows
    part = w_gate.shape[1] // members
    wide = -(-part // 128) * 128
    down_rows = w_down.shape[0]
    down_wide = wide // teams
    down_shift = down_wide - down_rows

    half_qkv = qkv_cols // 2
    half_out = -(-model // 256) * 128
    half = half_qkv + half_out

    def halves(qkv_block, out_block):
        out_block = jnp.pad(out_block, ((0, 0),) * (out_block.ndim - 1) + ((0, 2 * half_out - model),))
        return jnp.stack(
            [
                jnp.concatenate(
                    [
                        qkv_block[..., c * half_qkv : (c + 1) * half_qkv],
                        out_block[..., c * half_out : (c + 1) * half_out],
                    ],
                    axis=-1,
                )
                for c in range(cores)
            ]
        )

    gains = (in_gain, query_gain, key_gain, post_attn_gain, pre_ff_gain, post_ff_gain)
    gain_row = jnp.concatenate(gains)
    gain_row = jnp.pad(gain_row, (0, model - gain_row.shape[0]))[None]
    attn_rows = halves(
        jnp.concatenate([w_query, w_key, w_value], axis=1),
        jnp.concatenate([w_out, gain_row], axis=0),
    )
    attn_rows = gather_blocks(attn_rows, "y").transpose(1, 0, 2, 3)
    attn_rows = swap(attn_rows, "core").reshape(members, rows, half)
    attn_shard = jnp.concatenate(
        [
            attn_rows[:, :, :half_qkv].reshape(team_rows, half_qkv),
            jnp.concatenate(
                [
                    attn_rows[:, :out_rows, half_qkv:].reshape(members * out_rows, half_out),
                    attn_rows[:, out_rows, half_qkv:],
                ],
                axis=0,
            ),
        ],
        axis=1,
    )
    attn_all = lax.all_gather(attn_shard, ("x", "z", "core"), axis=0, tiled=True)
    attn_all = attn_all.reshape(teams, cores, team_rows, half)
    full_qkv = jnp.concatenate(
        [attn_all[:, c, :, :half_qkv].reshape(model, half_qkv) for c in range(cores)], axis=1
    )
    full_out = jnp.concatenate(
        [
            attn_all[:, c, : members * out_rows, half_qkv:].reshape(query_cols, half_out)
            for c in range(cores)
        ],
        axis=1,
    )[:, :model]
    gain_all = attn_all[:, 0, members * out_rows :, half_qkv : half_qkv + 128].astype(f32)
    full_gains = []
    first = 0
    for item in gains:
        size = item.shape[0]
        full_gains.append(gain_all[:, :, first : first + size].reshape(-1))
        first += size
    gain_in, gain_query, gain_key, gain_post_attn, gain_pre, gain_post = full_gains

    def columns(weight):
        pieces = weight.reshape(rows, members, part)
        return jnp.pad(pieces, ((0, 0), (0, 0), (0, wide - part)))

    both = jnp.concatenate([columns(w_gate), columns(w_up)], axis=2).transpose(1, 0, 2)
    both = both.reshape(cores, inner, rows, 2 * wide)
    by_y = swap(both.transpose(1, 2, 0, 3).reshape(inner, rows, cores * 2 * wide), "y")
    by_core = by_y.reshape(inner, rows, cores, 2 * wide).transpose(2, 0, 1, 3)
    by_member = swap(by_core, "core").reshape(team_rows, 2 * wide)
    here, before = down_routes(teams, members)
    down_two = jnp.concatenate(
        [lax.ppermute(w_down, all_axes, here), lax.ppermute(w_down, all_axes, before)], axis=0
    )
    down_part = lax.dynamic_slice_in_dim(down_two, down_shift * team, down_wide, 0)
    filling = jnp.broadcast_to(attn_all[0, 0, 0, 0], (team_rows - down_wide, model))
    shard = jnp.concatenate(
        [by_member, jnp.concatenate([down_part, filling], axis=0)],
        axis=1,
    )
    full = lax.all_gather(shard, ("x", "z"), axis=0, tiled=True)
    full_both = full[:, : 2 * wide]
    full_down = full.reshape(teams, team_rows, -1)[:, :down_wide, 2 * wide :].reshape(wide, model)

    inputs = activations[0].astype(f32)
    segment_all = segments[0]
    tok_count = inputs.shape[0]
    first_place = me * tok_count
    place_rows = first_place + jnp.arange(tok_count, dtype=jnp.int32)
    segment_rows = lax.dynamic_slice_in_dim(segment_all, first_place, tok_count)
    earlier = jnp.sum((segment_all[None, :] < segment_rows[:, None]).astype(jnp.int32), axis=1)
    cosine, sine = rope_tables(place_rows - earlier, head_dim)
    length = segment_all.shape[0]
    key_places = (first_place + jnp.arange(length, dtype=jnp.int32)) % length
    key_segments = jnp.take(segment_all, key_places)
    allowed = (segment_rows[:, None] == key_segments[None, :]) & (
        place_rows[:, None] >= key_places[None, :]
    )
    allowed = jnp.tile(allowed, (heads, 1))

    normed, in_pull = jax.vjp(rms_norm, inputs, gain_in)
    normed_low = normed.astype(bf16)
    qkv = contract(normed_low, full_qkv, 1, 0)
    query_raw = qkv[:, :query_cols].reshape(tok_count, heads, head_dim)
    key_raw = qkv[:, query_cols : query_cols + head_dim]
    value_low = qkv[:, query_cols + head_dim :].astype(bf16)

    def prepare(query_in, key_in, query_scale, key_scale):
        rotated_query = rotate(
            rms_norm(query_in, query_scale), cosine[:, None, :], sine[:, None, :]
        )
        rotated_key = rotate(rms_norm(key_in, key_scale), cosine, sine)
        return (rotated_query, rotated_key)

    (queries, key_rows), prepare_pull = jax.vjp(prepare, query_raw, key_raw, gain_query, gain_key)
    query_low = queries.astype(bf16).transpose(1, 0, 2).reshape(heads * tok_count, head_dim)
    key_value = gather_ahead(jnp.concatenate([key_rows.astype(bf16), value_low], axis=1))
    key_all = key_value[:, :head_dim]
    value_all = key_value[:, head_dim:]

    scores = contract(query_low, key_all, 1, 1) * score_scale
    scores = jnp.where(allowed, scores, far_below)
    top_score = jnp.max(scores, axis=-1, keepdims=True)
    weight = jnp.exp(scores - top_score)
    prob = weight / jnp.sum(weight, axis=-1, keepdims=True)
    prob_low = prob.astype(bf16)
    attended = contract(prob_low, value_all, 1, 0).astype(bf16)
    attended_low = attended.reshape(heads, tok_count, head_dim).transpose(1, 0, 2)
    attended_low = attended_low.reshape(tok_count, query_cols)
    attn_out = contract(attended_low, full_out, 1, 0)
    post_attn, post_attn_pull = jax.vjp(rms_norm, attn_out, gain_post_attn)
    middle = inputs + post_attn
    normed_ff, pre_pull = jax.vjp(rms_norm, middle, gain_pre)
    normed_all = gather_team(normed_ff.astype(bf16))

    gate_up = contract(normed_all, full_both, 1, 0)
    mixed, gated_pull = jax.vjp(gated_unit, gate_up[:, :wide], gate_up[:, wide:])
    mixed_low = mixed.astype(bf16)
    branch_term = contract(mixed_low, full_down, 1, 0)
    branch_out = sum_team(branch_term, tok_count)
    post_ff, post_pull = jax.vjp(rms_norm, branch_out, gain_post)
    output = (middle + post_ff).astype(bf16)

    grad_output = cotangent[0].astype(f32)
    grad_branch, grad_post_ff = post_pull(grad_output)
    grad_branch_all = gather_team(grad_branch.astype(bf16))
    down_term = contract(mixed_low, grad_branch_all, 0, 0, bf16)
    grad_mixed = contract(grad_branch_all, full_down, 1, 1)
    grad_gate, grad_up = gated_pull(grad_mixed)
    grad_both = jnp.concatenate([grad_gate.astype(bf16), grad_up.astype(bf16)], axis=1)
    both_term = contract(normed_all, grad_both, 0, 0, bf16)
    grad_normed_term = contract(grad_both, full_both, 1, 1)
    ffn_terms = jnp.concatenate(
        [
            both_term.reshape(teams, team_rows, 2 * wide),
            jnp.pad(
                down_term.reshape(teams, down_wide, model),
                ((0, 0), (0, team_rows - down_wide), (0, 0)),
            ),
        ],
        axis=2,
    ).reshape(teams * team_rows, -1)
    ffn_terms, grad_normed_term = lax.optimization_barrier((ffn_terms, grad_normed_term))
    ffn_sum = lax.psum_scatter(ffn_terms.reshape(teams, team_rows, -1), ("x", "z"), scatter_dimension=0, tiled=True)[0]
    both_grad = ffn_sum[:, : 2 * wide].reshape(cores, inner, rows, 2 * wide).transpose(1, 0, 2, 3)
    both_grad = swap(both_grad, "y").transpose(1, 0, 2, 3)
    both_grad = swap(both_grad, "core").reshape(members, rows, 2 * wide).astype(f32)
    both_grad = both_grad.transpose(1, 0, 2)
    gate_grad = both_grad[:, :, :part].reshape(rows, members * part)
    up_grad = both_grad[:, :, wide : wide + part].reshape(rows, members * part)
    down_sum = ffn_sum[:down_wide, 2 * wide :]
    down_two = jnp.concatenate(
        [
            lax.ppermute(down_sum, all_axes, [(b, a) for a, b in before]),
            lax.ppermute(down_sum, all_axes, [(b, a) for a, b in here]),
        ],
        axis=0,
    )
    down_grad = lax.dynamic_slice_in_dim(
        down_two, down_wide - down_shift * (flat % teams), down_rows, 0
    ).astype(f32)

    grad_normed_ff = sum_team(grad_normed_term, tok_count)
    grad_middle_add, grad_pre_ff = pre_pull(grad_normed_ff)
    grad_middle = grad_output + grad_middle_add
    grad_attn, grad_post_attn = post_attn_pull(grad_middle)
    grad_attn_low = grad_attn.astype(bf16)
    out_term = contract(attended_low, grad_attn_low, 0, 0, bf16)
    grad_attended = contract(grad_attn_low, full_out, 1, 1, bf16)
    grad_attended = grad_attended.reshape(tok_count, heads, head_dim).transpose(1, 0, 2)
    grad_attended = grad_attended.reshape(heads * tok_count, head_dim)

    grad_prob = contract(grad_attended, value_all, 1, 1)
    shift_term = jnp.sum(prob * grad_prob, axis=-1, keepdims=True)
    grad_scores = (prob * (grad_prob - shift_term)).astype(bf16)
    grad_query = contract(grad_scores, key_all, 1, 0) * score_scale
    grad_key = contract(grad_scores, query_low, 0, 0) * score_scale
    grad_value = contract(prob_low, grad_attended, 0, 0)
    grad_key_value = jnp.concatenate([grad_key, grad_value], axis=1)
    grad_key_value = sum_ahead(
        [grad_key_value[s * tok_count : (s + 1) * tok_count] for s in range(inner)]
    )
    grad_queries = grad_query.reshape(heads, tok_count, head_dim).transpose(1, 0, 2)
    grad_query_raw, grad_key_raw, grad_query_gain, grad_key_gain = prepare_pull(
        (grad_queries, grad_key_value[:, :head_dim])
    )
    grad_qkv = jnp.concatenate(
        [
            grad_query_raw.reshape(tok_count, query_cols),
            grad_key_raw,
            grad_key_value[:, head_dim:],
        ],
        axis=1,
    ).astype(bf16)
    qkv_term = contract(normed_low, grad_qkv, 0, 0, bf16)
    grad_normed = contract(grad_qkv, full_qkv, 1, 1)
    grad_input_add, grad_in_gain = in_pull(grad_normed)
    input_grad = grad_middle + grad_input_add

    grad_gains = (
        grad_in_gain,
        grad_query_gain,
        grad_key_gain,
        grad_post_attn,
        grad_pre_ff,
        grad_post_ff,
    )
    gain_terms = jnp.concatenate(
        [item.reshape(teams, members, -1) for item in grad_gains], axis=2
    ).astype(bf16)
    gain_terms = jnp.pad(gain_terms, ((0, 0), (0, 0), (0, model - gain_terms.shape[2])))
    attn_terms = halves(
        qkv_term.reshape(teams, team_rows, qkv_cols),
        jnp.concatenate(
            [out_term.reshape(teams, members * out_rows, model), gain_terms], axis=1
        ),
    )
    attn_half = reduce_axis(attn_terms, "core", 0)
    attn_half = attn_half.reshape(lax.axis_size("x"), lax.axis_size("z"), team_rows, half)
    left = reduce_axis(attn_half[..., :half_qkv], "x", 0)
    right = reduce_axis(attn_half[..., half_qkv:], "z", 1)
    left = reduce_axis(left, "z", 0)
    right = reduce_axis(right, "x", 0)
    attn_sum = jnp.concatenate(
        [
            left.reshape(members, rows, half_qkv),
            jnp.concatenate(
                [
                    right[: members * out_rows].reshape(members, out_rows, half_out),
                    right[members * out_rows :][:, None],
                ],
                axis=1,
            ),
        ],
        axis=2,
    ).reshape(cores, inner, rows, half)
    attn_sum = swap(reduce_axis(attn_sum, "y", 1), "core").astype(f32)
    attn_grad = jnp.concatenate(
        [attn_sum[c, :, :half_qkv] for c in range(cores)]
        + [attn_sum[c, :, half_qkv:] for c in range(cores)],
        axis=1,
    )
    gain_grads = []
    first = qkv_cols
    for item in gains:
        size = item.shape[0]
        gain_grads.append(attn_grad[rows - 1, first : first + size])
        first += size
    return (
        output[None],
        input_grad[None],
        *gain_grads,
        attn_grad[:, :query_cols],
        attn_grad[:, query_cols : query_cols + head_dim],
        attn_grad[:, query_cols + head_dim : qkv_cols],
        attn_grad[:out_rows, qkv_cols : qkv_cols + model],
        gate_grad,
        up_grad,
        down_grad,
    )


def solution(mesh):
    fine = Mesh(mesh.devices.reshape(4, 4, 2, 4), ("x", "z", "core", "y"))
    all_axes = ("x", "z", "core", "y")
    shard = P(all_axes)
    matrix = P(all_axes, None)
    tokens = P(("x", "z", "core"), "y", None)
    return jax.shard_map(
        local,
        mesh=fine,
        in_specs=(tokens, tokens, P(("x", "z", "core"), None)) + (shard,) * 6 + (matrix,) * 7,
        out_specs=(tokens, tokens) + (shard,) * 6 + (matrix,) * 7,
        check_vma=False,
    )
```

```python
import math

import jax
import jax.numpy as jnp
from jax import lax
from jax.sharding import Mesh
from jax.sharding import PartitionSpec as P

norm_eps = 1e-06
rope_base = 1000000.0
score_scale = 0.0625
far_below = -1e30
f32 = jnp.float32
bf16 = jnp.bfloat16


def rms_norm(values, gain):
    factor = lax.rsqrt(jnp.mean(values * values, axis=-1, keepdims=True) + norm_eps)
    return values * factor * (1.0 + gain)


def rotate(values, cosine, sine):
    half_dim = values.shape[-1] // 2
    first_half = values[..., :half_dim]
    second_half = values[..., half_dim:]
    return jnp.concatenate(
        [first_half * cosine - second_half * sine, second_half * cosine + first_half * sine],
        axis=-1,
    )


def rope_tables(positions, head_dim):
    freq_index = jnp.arange(head_dim // 2, dtype=f32)
    inverse = jnp.exp(freq_index * (-2.0 / head_dim) * math.log(rope_base))
    angles = positions.astype(f32)[:, None] * inverse[None, :]
    return (jnp.cos(angles), jnp.sin(angles))


def gated_unit(gate_pre, up_pre):
    return jax.nn.gelu(gate_pre, approximate=True) * up_pre


def contract(left, right, left_dim, right_dim, kind=f32):
    return lax.dot_general(
        left, right, (((left_dim,), (right_dim,)), ((), ())), preferred_element_type=kind
    )


def from_ahead(block, step, axis="y"):
    size = lax.axis_size(axis)
    return lax.ppermute(block, axis, [(i, (i - step) % size) for i in range(size)])


def to_ahead(block, step, axis="y"):
    size = lax.axis_size(axis)
    return lax.ppermute(block, axis, [(i, (i + step) % size) for i in range(size)])


def gather_ahead(block, axis="y"):
    size = lax.axis_size(axis)
    return jnp.concatenate([block] + [from_ahead(block, s, axis) for s in range(1, size)], axis=0)


def sum_ahead(terms, axis="y"):
    arrived = [to_ahead(terms[s].astype(bf16), s, axis) for s in range(1, len(terms))]
    total = terms[0].astype(f32)
    for item in arrived:
        total = total + item.astype(f32)
    return total


def swap(pieces, axis):
    size = lax.axis_size(axis)
    me = lax.axis_index(axis)
    arrived = [lax.dynamic_index_in_dim(pieces, me, 0, keepdims=False)]
    for s in range(1, size):
        item = lax.dynamic_index_in_dim(pieces, (me + s) % size, 0, keepdims=False)
        arrived.append(to_ahead(item, s, axis))
    return by_sender(arrived, axis)


def by_sender(arrived, axis):
    size = lax.axis_size(axis)
    me = lax.axis_index(axis)
    result = []
    for c in range(size):
        item = arrived[0]
        for s in range(1, size):
            item = jnp.where((me - c) % size == s, arrived[s], item)
        result.append(item)
    return jnp.stack(result)


def reduce_axis(terms, axis, dim):
    size = lax.axis_size(axis)
    me = lax.axis_index(axis)
    total = lax.dynamic_index_in_dim(terms, me, dim, keepdims=False).astype(f32)
    arrived = [
        to_ahead(lax.dynamic_index_in_dim(terms, (me + s) % size, dim, keepdims=False), s, axis)
        for s in range(1, size)
    ]
    for item in arrived:
        total = total + item.astype(f32)
    return total.astype(bf16)


def side_by_side(items, width):
    total, first = None, 0
    for item in items:
        last = width - first - item.shape[-1]
        placed = jnp.pad(item, ((0, 0),) * (item.ndim - 1) + ((first, last),))
        total = placed if total is None else total + placed
        first += item.shape[-1]
    return total


def gather_blocks(block, axis):
    size = lax.axis_size(axis)
    return by_sender([block] + [to_ahead(block, s, axis) for s in range(1, size)], axis)


def gather_team(block):
    return gather_ahead(gather_ahead(block, "y"), "core")


def sum_team(term, tokens):
    half = term.shape[0] // 2
    term = sum_ahead([term[:half], term[half:]], "core")
    return sum_ahead([term[i : i + tokens] for i in range(0, half, tokens)], "y")


def down_routes(teams, members):
    here, before = [], []
    for member in range(members):
        for block in range(teams):
            owner = member * teams + block
            here.append((owner, block * members + member))
            if block > 0:
                before.append((owner, (block - 1) * members + member))
    return here, before


def local(
    activations,
    cotangent,
    segments,
    in_gain,
    query_gain,
    key_gain,
    post_attn_gain,
    pre_ff_gain,
    post_ff_gain,
    w_query,
    w_key,
    w_value,
    w_out,
    w_gate,
    w_up,
    w_down,
):
    all_axes = ("x", "z", "core", "y")
    teams = lax.axis_size("x") * lax.axis_size("z")
    inner = lax.axis_size("y")
    cores = lax.axis_size("core")
    members = inner * cores
    me = lax.axis_index("y")
    team = lax.axis_index("x") * lax.axis_size("z") + lax.axis_index("z")
    flat = team * members + lax.axis_index("core") * inner + me
    rows = w_query.shape[0]
    model = w_down.shape[1]
    query_cols = w_query.shape[1]
    head_dim = w_key.shape[1]
    heads = query_cols // head_dim
    qkv_cols = query_cols + 2 * head_dim
    out_rows = w_out.shape[0]
    team_rows = members * rows
    part = w_gate.shape[1] // members
    wide = -(-part // 128) * 128
    down_rows = w_down.shape[0]
    down_wide = wide // teams
    down_shift = down_wide - down_rows

    half_qkv = qkv_cols // 2
    half_out = -(-model // 256) * 128
    half = half_qkv + half_out

    def halves(qkv_block, out_block):
        out_block = jnp.pad(out_block, ((0, 0),) * (out_block.ndim - 1) + ((0, 2 * half_out - model),))
        return jnp.stack(
            [
                jnp.concatenate(
                    [
                        qkv_block[..., c * half_qkv : (c + 1) * half_qkv],
                        out_block[..., c * half_out : (c + 1) * half_out],
                    ],
                    axis=-1,
                )
                for c in range(cores)
            ]
        )

    gains = (in_gain, query_gain, key_gain, post_attn_gain, pre_ff_gain, post_ff_gain)
    gain_row = side_by_side(gains, model)[None]
    attn_rows = halves(
        jnp.concatenate([w_query, w_key, w_value], axis=1),
        jnp.concatenate([w_out, gain_row], axis=0),
    )
    attn_rows = gather_blocks(attn_rows, "y").transpose(1, 0, 2, 3)
    attn_rows = swap(attn_rows, "core").reshape(members, rows, half)
    attn_shard = jnp.concatenate(
        [
            attn_rows[:, :, :half_qkv].reshape(team_rows, half_qkv),
            jnp.concatenate(
                [
                    attn_rows[:, :out_rows, half_qkv:].reshape(members * out_rows, half_out),
                    attn_rows[:, out_rows, half_qkv:],
                ],
                axis=0,
            ),
        ],
        axis=1,
    )
    attn_mine = lax.all_gather(attn_shard, ("x", "z"), axis=0, tiled=True)
    attn_mine = attn_mine.reshape(teams, team_rows, half)
    attn_other = to_ahead(attn_mine, 1, "core")
    is_first = lax.axis_index("core") == 0

    def in_order(one, two):
        return jnp.where(is_first, one, two), jnp.where(is_first, two, one)

    qkv_mine, qkv_other = (
        item[:, :, :half_qkv].reshape(model, half_qkv) for item in (attn_mine, attn_other)
    )
    out_mine, out_other = (
        item[:, : members * out_rows, half_qkv:].reshape(query_cols, half_out)
        for item in (attn_mine, attn_other)
    )
    gain_all = in_order(
        *(
            item[:, members * out_rows :, half_qkv : half_qkv + 128].astype(f32)
            for item in (attn_mine, attn_other)
        )
    )[0]
    full_gains = []
    first = 0
    for item in gains:
        size = item.shape[0]
        full_gains.append(gain_all[:, :, first : first + size].reshape(-1))
        first += size
    gain_in, gain_query, gain_key, gain_post_attn, gain_pre, gain_post = full_gains

    def columns(weight):
        pieces = weight.reshape(rows, members, part)
        return jnp.pad(pieces, ((0, 0), (0, 0), (0, wide - part)))

    both = jnp.concatenate([columns(w_gate), columns(w_up)], axis=2).transpose(1, 0, 2)
    both = both.reshape(cores, inner, rows, 2 * wide)
    by_y = swap(both.transpose(1, 2, 0, 3).reshape(inner, rows, cores * 2 * wide), "y")
    by_core = by_y.reshape(inner, rows, cores, 2 * wide).transpose(2, 0, 1, 3)
    by_member = swap(by_core, "core").reshape(team_rows, 2 * wide)
    here, before = down_routes(teams, members)
    down_two = jnp.concatenate(
        [lax.ppermute(w_down, all_axes, here), lax.ppermute(w_down, all_axes, before)], axis=0
    )
    down_part = lax.dynamic_slice_in_dim(down_two, down_shift * team, down_wide, 0)
    filling = jnp.broadcast_to(attn_mine[0, 0, 0], (team_rows - down_wide, model))
    shard = jnp.concatenate(
        [by_member, jnp.concatenate([down_part, filling], axis=0)],
        axis=1,
    )
    full = lax.all_gather(shard, ("x", "z"), axis=0, tiled=True)
    full_both = full[:, : 2 * wide]
    full_down = full.reshape(teams, team_rows, -1)[:, :down_wide, 2 * wide :].reshape(wide, model)

    inputs = activations[0].astype(f32)
    segment_all = segments[0]
    tok_count = inputs.shape[0]
    first_place = me * tok_count
    place_rows = first_place + jnp.arange(tok_count, dtype=jnp.int32)
    segment_rows = lax.dynamic_slice_in_dim(segment_all, first_place, tok_count)
    earlier = jnp.sum((segment_all[None, :] < segment_rows[:, None]).astype(jnp.int32), axis=1)
    cosine, sine = rope_tables(place_rows - earlier, head_dim)
    length = segment_all.shape[0]
    key_places = (first_place + jnp.arange(length, dtype=jnp.int32)) % length
    key_segments = jnp.take(segment_all, key_places)
    allowed = (segment_rows[:, None] == key_segments[None, :]) & (
        place_rows[:, None] >= key_places[None, :]
    )
    allowed = jnp.tile(allowed, (heads, 1))

    normed, in_pull = jax.vjp(rms_norm, inputs, gain_in)
    normed_low = normed.astype(bf16)
    qkv = jnp.concatenate(
        in_order(contract(normed_low, qkv_mine, 1, 0), contract(normed_low, qkv_other, 1, 0)),
        axis=1,
    )
    query_raw = qkv[:, :query_cols].reshape(tok_count, heads, head_dim)
    key_raw = qkv[:, query_cols : query_cols + head_dim]
    value_low = qkv[:, query_cols + head_dim :].astype(bf16)

    def prepare(query_in, key_in, query_scale, key_scale):
        rotated_query = rotate(
            rms_norm(query_in, query_scale), cosine[:, None, :], sine[:, None, :]
        )
        rotated_key = rotate(rms_norm(key_in, key_scale), cosine, sine)
        return (rotated_query, rotated_key)

    (queries, key_rows), prepare_pull = jax.vjp(prepare, query_raw, key_raw, gain_query, gain_key)
    query_low = queries.astype(bf16).transpose(1, 0, 2).reshape(heads * tok_count, head_dim)
    key_value = gather_ahead(jnp.concatenate([key_rows.astype(bf16), value_low], axis=1))
    key_all = key_value[:, :head_dim]
    value_all = key_value[:, head_dim:]

    scores = contract(query_low, key_all, 1, 1) * score_scale
    scores = jnp.where(allowed, scores, far_below)
    top_score = jnp.max(scores, axis=-1, keepdims=True)
    weight = jnp.exp(scores - top_score)
    prob = weight / jnp.sum(weight, axis=-1, keepdims=True)
    prob_low = prob.astype(bf16)
    attended = contract(prob_low, value_all, 1, 0).astype(bf16)
    attended_low = attended.reshape(heads, tok_count, head_dim).transpose(1, 0, 2)
    attended_low = attended_low.reshape(tok_count, query_cols)
    attn_out = jnp.concatenate(
        in_order(contract(attended_low, out_mine, 1, 0), contract(attended_low, out_other, 1, 0)),
        axis=1,
    )[:, :model]
    post_attn, post_attn_pull = jax.vjp(rms_norm, attn_out, gain_post_attn)
    middle = inputs + post_attn
    normed_ff, pre_pull = jax.vjp(rms_norm, middle, gain_pre)
    normed_all = gather_team(normed_ff.astype(bf16))

    gate_up = contract(normed_all, full_both, 1, 0)
    mixed, gated_pull = jax.vjp(gated_unit, gate_up[:, :wide], gate_up[:, wide:])
    mixed_low = mixed.astype(bf16)
    team_half = inner * tok_count
    branch_other = to_ahead(contract(mixed_low[team_half:], full_down, 1, 0, bf16), 1, "core")
    branch_term = contract(mixed_low[:team_half], full_down, 1, 0) + branch_other.astype(f32)
    branch_out = sum_ahead(
        [branch_term[i : i + tok_count] for i in range(0, team_half, tok_count)], "y"
    )
    post_ff, post_pull = jax.vjp(rms_norm, branch_out, gain_post)
    output = (middle + post_ff).astype(bf16)

    grad_output = cotangent[0].astype(f32)
    grad_branch, grad_post_ff = post_pull(grad_output)
    grad_branch_all = gather_team(grad_branch.astype(bf16))
    grad_mixed = contract(grad_branch_all, full_down, 1, 1)
    grad_gate, grad_up = gated_pull(grad_mixed)
    grad_both = jnp.concatenate([grad_gate.astype(bf16), grad_up.astype(bf16)], axis=1)
    grad_normed_term = contract(grad_both, full_both, 1, 1)
    grad_both, mixed_low, grad_normed_term = lax.optimization_barrier(
        (grad_both, mixed_low, grad_normed_term)
    )
    grad_normed_ff = sum_team(grad_normed_term, tok_count)
    down_term = contract(mixed_low, grad_branch_all, 0, 0, bf16)
    both_term = contract(normed_all, grad_both, 0, 0, bf16)
    ffn_terms = jnp.concatenate(
        [
            both_term.reshape(teams, team_rows, 2 * wide),
            jnp.pad(
                down_term.reshape(teams, down_wide, model),
                ((0, 0), (0, team_rows - down_wide), (0, 0)),
            ),
        ],
        axis=2,
    ).reshape(teams * team_rows, -1)
    ffn_terms, grad_normed_ff = lax.optimization_barrier((ffn_terms, grad_normed_ff))
    ffn_sum = lax.psum_scatter(ffn_terms.reshape(teams, team_rows, -1), ("x", "z"), scatter_dimension=0, tiled=True)[0]
    down_sum = ffn_sum[:down_wide, 2 * wide :]
    down_two = jnp.concatenate(
        [
            lax.ppermute(down_sum, all_axes, [(b, a) for a, b in before]),
            lax.ppermute(down_sum, all_axes, [(b, a) for a, b in here]),
        ],
        axis=0,
    )
    down_grad = lax.dynamic_slice_in_dim(
        down_two, down_wide - down_shift * (flat % teams), down_rows, 0
    ).astype(f32)

    grad_middle_add, grad_pre_ff = pre_pull(grad_normed_ff)
    grad_middle = grad_output + grad_middle_add
    grad_attn, grad_post_attn = post_attn_pull(grad_middle)
    grad_attn_low = grad_attn.astype(bf16)
    grad_attn_mine, grad_attn_other = in_order(
        grad_attn_low[:, :half_out],
        jnp.pad(grad_attn_low[:, half_out:], ((0, 0), (0, 2 * half_out - model))),
    )
    grad_attended = (
        contract(grad_attn_mine, out_mine, 1, 1) + contract(grad_attn_other, out_other, 1, 1)
    ).astype(bf16)
    grad_attended = grad_attended.reshape(tok_count, heads, head_dim).transpose(1, 0, 2)
    grad_attended = grad_attended.reshape(heads * tok_count, head_dim)

    grad_prob = contract(grad_attended, value_all, 1, 1)
    shift_term = jnp.sum(prob * grad_prob, axis=-1, keepdims=True)
    grad_scores = (prob * (grad_prob - shift_term)).astype(bf16)
    grad_query = contract(grad_scores, key_all, 1, 0) * score_scale
    grad_key = contract(grad_scores, query_low, 0, 0) * score_scale
    grad_value = contract(prob_low, grad_attended, 0, 0)
    grad_key_value = jnp.concatenate([grad_key, grad_value], axis=1)
    grad_key_value = sum_ahead(
        [grad_key_value[s * tok_count : (s + 1) * tok_count] for s in range(inner)]
    )
    grad_queries = grad_query.reshape(heads, tok_count, head_dim).transpose(1, 0, 2)
    grad_query_raw, grad_key_raw, grad_query_gain, grad_key_gain = prepare_pull(
        (grad_queries, grad_key_value[:, :head_dim])
    )
    grad_qkv = jnp.concatenate(
        [
            grad_query_raw.reshape(tok_count, query_cols),
            grad_key_raw,
            grad_key_value[:, head_dim:],
        ],
        axis=1,
    ).astype(bf16)
    grad_qkv_mine, grad_qkv_other = in_order(grad_qkv[:, :half_qkv], grad_qkv[:, half_qkv:])
    grad_normed = contract(grad_qkv_mine, qkv_mine, 1, 1) + contract(
        grad_qkv_other, qkv_other, 1, 1
    )
    grad_input_add, grad_in_gain = in_pull(grad_normed)
    input_grad = grad_middle + grad_input_add

    grad_gains = (
        grad_in_gain,
        grad_query_gain,
        grad_key_gain,
        grad_post_attn,
        grad_pre_ff,
        grad_post_ff,
    )
    gain_terms = side_by_side(
        [item.reshape(teams, members, -1) for item in grad_gains], half_out
    ).astype(bf16)

    def half_terms(grad_qkv_half, grad_attn_half, gain_half):
        qkv_term = contract(normed_low, grad_qkv_half, 0, 0, bf16)
        out_term = contract(attended_low, grad_attn_half, 0, 0, bf16)
        out_term = out_term.reshape(teams, members * out_rows, half_out)
        return jnp.concatenate(
            [
                qkv_term.reshape(teams, team_rows, half_qkv),
                jnp.concatenate([out_term, gain_half], axis=1),
            ],
            axis=2,
        )

    gain_mine, gain_other = in_order(gain_terms, jnp.zeros_like(gain_terms))
    term_other = to_ahead(half_terms(grad_qkv_other, grad_attn_other, gain_other), 1, "core")
    term_mine = half_terms(grad_qkv_mine, grad_attn_mine, gain_mine)
    attn_half = (term_mine.astype(f32) + term_other.astype(f32)).astype(bf16)
    attn_half = attn_half.reshape(lax.axis_size("x"), lax.axis_size("z"), team_rows, half)
    left = reduce_axis(attn_half[..., :half_qkv], "x", 0)
    right = reduce_axis(attn_half[..., half_qkv:], "z", 1)
    left = reduce_axis(left, "z", 0)
    right = reduce_axis(right, "x", 0)
    attn_sum = jnp.concatenate(
        [
            left.reshape(members, rows, half_qkv),
            jnp.concatenate(
                [
                    right[: members * out_rows].reshape(members, out_rows, half_out),
                    right[members * out_rows :][:, None],
                ],
                axis=1,
            ),
        ],
        axis=2,
    ).reshape(cores, inner, rows, half)
    message = jnp.concatenate(
        [
            ffn_sum[:, : 2 * wide].reshape(cores, inner, rows, 2 * wide),
            attn_sum,
        ],
        axis=3,
    ).transpose(1, 0, 2, 3)
    by_y = swap(message, "y")
    attn_sum = jnp.sum(by_y[..., 2 * wide :].astype(f32), axis=0).astype(bf16)
    message = jnp.concatenate(
        [by_y[c, :, :, : 2 * wide] for c in range(inner)] + [attn_sum], axis=2
    )
    by_core = swap(message, "core").astype(f32)
    both_grad = jnp.concatenate(
        [
            by_core[c, None, :, k * 2 * wide : (k + 1) * 2 * wide]
            for c in range(cores)
            for k in range(inner)
        ],
        axis=0,
    ).transpose(1, 0, 2)
    gate_grad = both_grad[:, :, :part].reshape(rows, members * part)
    up_grad = both_grad[:, :, wide : wide + part].reshape(rows, members * part)
    attn_sum = by_core[:, :, inner * 2 * wide :]
    attn_grad = jnp.concatenate(
        [attn_sum[c, :, :half_qkv] for c in range(cores)]
        + [attn_sum[c, :, half_qkv:] for c in range(cores)],
        axis=1,
    )
    gain_grads = []
    first = qkv_cols
    for item in gains:
        size = item.shape[0]
        gain_grads.append(attn_grad[rows - 1, first : first + size])
        first += size
    return (
        output[None],
        input_grad[None],
        *gain_grads,
        attn_grad[:, :query_cols],
        attn_grad[:, query_cols : query_cols + head_dim],
        attn_grad[:, query_cols + head_dim : qkv_cols],
        attn_grad[:out_rows, qkv_cols : qkv_cols + model],
        gate_grad,
        up_grad,
        down_grad,
    )


def solution(mesh):
    fine = Mesh(mesh.devices.reshape(4, 4, 2, 4), ("x", "z", "core", "y"))
    all_axes = ("x", "z", "core", "y")
    shard = P(all_axes)
    matrix = P(all_axes, None)
    tokens = P(("x", "z", "core"), "y", None)
    return jax.shard_map(
        local,
        mesh=fine,
        in_specs=(tokens, tokens, P(("x", "z", "core"), None)) + (shard,) * 6 + (matrix,) * 7,
        out_specs=(tokens, tokens) + (shard,) * 6 + (matrix,) * 7,
        check_vma=False,
    )
```

```python
import math

import jax
import jax.numpy as jnp
from jax import lax
from jax.sharding import Mesh
from jax.sharding import PartitionSpec as P

norm_eps = 1e-06
rope_base = 1000000.0
score_scale = 0.0625
far_below = -1e30
f32 = jnp.float32
bf16 = jnp.bfloat16


def rms_norm(values, gain):
    factor = lax.rsqrt(jnp.mean(values * values, axis=-1, keepdims=True) + norm_eps)
    return values * factor * (1.0 + gain)


def rotate(values, cosine, sine):
    half_dim = values.shape[-1] // 2
    first_half = values[..., :half_dim]
    second_half = values[..., half_dim:]
    return jnp.concatenate(
        [first_half * cosine - second_half * sine, second_half * cosine + first_half * sine],
        axis=-1,
    )


def rope_tables(positions, head_dim):
    freq_index = jnp.arange(head_dim // 2, dtype=f32)
    inverse = jnp.exp(freq_index * (-2.0 / head_dim) * math.log(rope_base))
    angles = positions.astype(f32)[:, None] * inverse[None, :]
    return (jnp.cos(angles), jnp.sin(angles))


def gated_unit(gate_pre, up_pre):
    return jax.nn.gelu(gate_pre, approximate=True) * up_pre


def contract(left, right, left_dim, right_dim, kind=f32):
    return lax.dot_general(
        left, right, (((left_dim,), (right_dim,)), ((), ())), preferred_element_type=kind
    )


def from_ahead(block, step, axis="y"):
    size = lax.axis_size(axis)
    return lax.ppermute(block, axis, [(i, (i - step) % size) for i in range(size)])


def to_ahead(block, step, axis="y"):
    size = lax.axis_size(axis)
    return lax.ppermute(block, axis, [(i, (i + step) % size) for i in range(size)])


def gather_ahead(block, axis="y"):
    size = lax.axis_size(axis)
    return jnp.concatenate([block] + [from_ahead(block, s, axis) for s in range(1, size)], axis=0)


def sum_ahead(terms, axis="y"):
    arrived = [to_ahead(terms[s].astype(bf16), s, axis) for s in range(1, len(terms))]
    total = terms[0].astype(f32)
    for item in arrived:
        total = total + item.astype(f32)
    return total


def swap(pieces, axis):
    size = lax.axis_size(axis)
    me = lax.axis_index(axis)
    arrived = [lax.dynamic_index_in_dim(pieces, me, 0, keepdims=False)]
    for s in range(1, size):
        item = lax.dynamic_index_in_dim(pieces, (me + s) % size, 0, keepdims=False)
        arrived.append(to_ahead(item, s, axis))
    return by_sender(arrived, axis)


def by_sender(arrived, axis):
    size = lax.axis_size(axis)
    me = lax.axis_index(axis)
    result = []
    for c in range(size):
        item = arrived[0]
        for s in range(1, size):
            item = jnp.where((me - c) % size == s, arrived[s], item)
        result.append(item)
    return jnp.stack(result)


def reduce_axis(terms, axis, dim):
    size = lax.axis_size(axis)
    me = lax.axis_index(axis)
    total = lax.dynamic_index_in_dim(terms, me, dim, keepdims=False).astype(f32)
    arrived = [
        to_ahead(lax.dynamic_index_in_dim(terms, (me + s) % size, dim, keepdims=False), s, axis)
        for s in range(1, size)
    ]
    for item in arrived:
        total = total + item.astype(f32)
    return total.astype(bf16)


def side_by_side(items, width):
    total, first = None, 0
    for item in items:
        last = width - first - item.shape[-1]
        placed = jnp.pad(item, ((0, 0),) * (item.ndim - 1) + ((first, last),))
        total = placed if total is None else total + placed
        first += item.shape[-1]
    return total


def gather_blocks(block, axis):
    size = lax.axis_size(axis)
    return by_sender([block] + [to_ahead(block, s, axis) for s in range(1, size)], axis)


def gather_team(block):
    return gather_ahead(gather_ahead(block, "y"), "core")


def sum_team(term, tokens):
    half = term.shape[0] // 2
    term = sum_ahead([term[:half], term[half:]], "core")
    return sum_ahead([term[i : i + tokens] for i in range(0, half, tokens)], "y")


def down_routes(teams, members):
    here, before = [], []
    for member in range(members):
        for block in range(teams):
            owner = member * teams + block
            here.append((owner, block * members + member))
            if block > 0:
                before.append((owner, (block - 1) * members + member))
    return here, before


def local(
    activations,
    cotangent,
    segments,
    in_gain,
    query_gain,
    key_gain,
    post_attn_gain,
    pre_ff_gain,
    post_ff_gain,
    w_query,
    w_key,
    w_value,
    w_out,
    w_gate,
    w_up,
    w_down,
):
    all_axes = ("x", "z", "core", "y")
    teams = lax.axis_size("x") * lax.axis_size("z")
    inner = lax.axis_size("y")
    cores = lax.axis_size("core")
    members = inner * cores
    me = lax.axis_index("y")
    team = lax.axis_index("x") * lax.axis_size("z") + lax.axis_index("z")
    flat = team * members + lax.axis_index("core") * inner + me
    rows = w_query.shape[0]
    model = w_down.shape[1]
    query_cols = w_query.shape[1]
    head_dim = w_key.shape[1]
    heads = query_cols // head_dim
    qkv_cols = query_cols + 2 * head_dim
    out_rows = w_out.shape[0]
    team_rows = members * rows
    part = w_gate.shape[1] // members
    wide = -(-part // 128) * 128
    down_rows = w_down.shape[0]
    down_wide = wide // teams
    down_shift = down_wide - down_rows

    half_qkv = qkv_cols // 2
    half_out = -(-model // 256) * 128
    half = half_qkv + half_out

    def halves(qkv_block, out_block):
        out_block = jnp.pad(out_block, ((0, 0),) * (out_block.ndim - 1) + ((0, 2 * half_out - model),))
        return jnp.stack(
            [
                jnp.concatenate(
                    [
                        qkv_block[..., c * half_qkv : (c + 1) * half_qkv],
                        out_block[..., c * half_out : (c + 1) * half_out],
                    ],
                    axis=-1,
                )
                for c in range(cores)
            ]
        )

    gains = (in_gain, query_gain, key_gain, post_attn_gain, pre_ff_gain, post_ff_gain)
    gain_row = side_by_side(gains, model)[None]
    attn_rows = halves(
        jnp.concatenate([w_query, w_key, w_value], axis=1),
        jnp.concatenate([w_out, gain_row], axis=0),
    )
    attn_rows = gather_blocks(attn_rows, "y").transpose(1, 0, 2, 3)
    attn_rows = swap(attn_rows, "core").reshape(members, rows, half)
    attn_shard = jnp.concatenate(
        [
            attn_rows[:, :, :half_qkv].reshape(team_rows, half_qkv),
            jnp.concatenate(
                [
                    attn_rows[:, :out_rows, half_qkv:].reshape(members * out_rows, half_out),
                    attn_rows[:, out_rows, half_qkv:],
                ],
                axis=0,
            ),
        ],
        axis=1,
    )
    attn_all = lax.all_gather(attn_shard, ("x", "z", "core"), axis=0, tiled=True)
    attn_all = attn_all.reshape(teams, cores, team_rows, half)
    full_qkv = jnp.concatenate(
        [attn_all[:, c, :, :half_qkv].reshape(model, half_qkv) for c in range(cores)], axis=1
    )
    full_out = jnp.concatenate(
        [
            attn_all[:, c, : members * out_rows, half_qkv:].reshape(query_cols, half_out)
            for c in range(cores)
        ],
        axis=1,
    )[:, :model]
    gain_all = attn_all[:, 0, members * out_rows :, half_qkv : half_qkv + 128].astype(f32)
    full_gains = []
    first = 0
    for item in gains:
        size = item.shape[0]
        full_gains.append(gain_all[:, :, first : first + size].reshape(-1))
        first += size
    gain_in, gain_query, gain_key, gain_post_attn, gain_pre, gain_post = full_gains

    def columns(weight):
        pieces = weight.reshape(rows, members, part)
        return jnp.pad(pieces, ((0, 0), (0, 0), (0, wide - part)))

    both = jnp.concatenate([columns(w_gate), columns(w_up)], axis=2).transpose(1, 0, 2)
    both = both.reshape(cores, inner, rows, 2 * wide)
    by_y = swap(both.transpose(1, 2, 0, 3).reshape(inner, rows, cores * 2 * wide), "y")
    by_core = by_y.reshape(inner, rows, cores, 2 * wide).transpose(2, 0, 1, 3)
    by_member = swap(by_core, "core").reshape(team_rows, 2 * wide)
    here, before = down_routes(teams, members)
    down_two = jnp.concatenate(
        [lax.ppermute(w_down, all_axes, here), lax.ppermute(w_down, all_axes, before)], axis=0
    )
    down_part = lax.dynamic_slice_in_dim(down_two, down_shift * team, down_wide, 0)
    filling = jnp.broadcast_to(attn_all[0, 0, 0, 0], (team_rows - down_wide, model))
    shard = jnp.concatenate(
        [by_member, jnp.concatenate([down_part, filling], axis=0)],
        axis=1,
    )
    full = lax.all_gather(shard, ("x", "z"), axis=0, tiled=True)
    full_both = full[:, : 2 * wide]
    full_down = full.reshape(teams, team_rows, -1)[:, :down_wide, 2 * wide :].reshape(wide, model)

    inputs = activations[0].astype(f32)
    segment_all = segments[0]
    tok_count = inputs.shape[0]
    first_place = me * tok_count
    place_rows = first_place + jnp.arange(tok_count, dtype=jnp.int32)
    segment_rows = lax.dynamic_slice_in_dim(segment_all, first_place, tok_count)
    earlier = jnp.sum((segment_all[None, :] < segment_rows[:, None]).astype(jnp.int32), axis=1)
    cosine, sine = rope_tables(place_rows - earlier, head_dim)
    length = segment_all.shape[0]
    key_places = (first_place + jnp.arange(length, dtype=jnp.int32)) % length
    key_segments = lax.dynamic_slice_in_dim(
        jnp.concatenate([segment_all, segment_all]), first_place, length
    )
    allowed = (segment_rows[:, None] == key_segments[None, :]) & (
        place_rows[:, None] >= key_places[None, :]
    )
    allowed = jnp.tile(allowed, (heads, 1))

    normed, in_pull = jax.vjp(rms_norm, inputs, gain_in)
    normed_low = normed.astype(bf16)
    qkv = contract(normed_low, full_qkv, 1, 0)
    query_raw = qkv[:, :query_cols].reshape(tok_count, heads, head_dim)
    key_raw = qkv[:, query_cols : query_cols + head_dim]
    value_low = qkv[:, query_cols + head_dim :].astype(bf16)

    def prepare(query_in, key_in, query_scale, key_scale):
        rotated_query = rotate(
            rms_norm(query_in, query_scale), cosine[:, None, :], sine[:, None, :]
        )
        rotated_key = rotate(rms_norm(key_in, key_scale), cosine, sine)
        return (rotated_query, rotated_key)

    (queries, key_rows), prepare_pull = jax.vjp(prepare, query_raw, key_raw, gain_query, gain_key)
    query_low = queries.astype(bf16).transpose(1, 0, 2).reshape(heads * tok_count, head_dim)
    key_value = gather_ahead(jnp.concatenate([key_rows.astype(bf16), value_low], axis=1))
    key_all = key_value[:, :head_dim]
    value_all = key_value[:, head_dim:]

    scores = contract(query_low, key_all, 1, 1) * score_scale
    scores = jnp.where(allowed, scores, far_below)
    top_score = jnp.max(scores, axis=-1, keepdims=True)
    weight = jnp.exp(scores - top_score)
    prob = weight / jnp.sum(weight, axis=-1, keepdims=True)
    prob_low = prob.astype(bf16)
    attended = contract(prob_low, value_all, 1, 0).astype(bf16)
    attended_low = attended.reshape(heads, tok_count, head_dim).transpose(1, 0, 2)
    attended_low = attended_low.reshape(tok_count, query_cols)
    attn_out = contract(attended_low, full_out, 1, 0)
    post_attn, post_attn_pull = jax.vjp(rms_norm, attn_out, gain_post_attn)
    middle = inputs + post_attn
    normed_ff, pre_pull = jax.vjp(rms_norm, middle, gain_pre)
    normed_all = gather_team(normed_ff.astype(bf16))

    gate_up = contract(normed_all, full_both, 1, 0)
    mixed, gated_pull = jax.vjp(gated_unit, gate_up[:, :wide], gate_up[:, wide:])
    mixed_low = mixed.astype(bf16)
    team_half = inner * tok_count
    branch_other = to_ahead(contract(mixed_low[team_half:], full_down, 1, 0, bf16), 1, "core")
    branch_term = contract(mixed_low[:team_half], full_down, 1, 0) + branch_other.astype(f32)
    branch_out = sum_ahead(
        [branch_term[i : i + tok_count] for i in range(0, team_half, tok_count)], "y"
    )
    post_ff, post_pull = jax.vjp(rms_norm, branch_out, gain_post)
    output = (middle + post_ff).astype(bf16)

    grad_output = cotangent[0].astype(f32)
    grad_branch, grad_post_ff = post_pull(grad_output)
    grad_branch_all = gather_team(grad_branch.astype(bf16))
    grad_mixed = contract(grad_branch_all, full_down, 1, 1)
    grad_gate, grad_up = gated_pull(grad_mixed)
    grad_both = jnp.concatenate([grad_gate.astype(bf16), grad_up.astype(bf16)], axis=1)
    grad_normed_term = contract(grad_both, full_both, 1, 1)
    grad_both, mixed_low, grad_normed_term = lax.optimization_barrier(
        (grad_both, mixed_low, grad_normed_term)
    )
    grad_normed_ff = sum_team(grad_normed_term, tok_count)
    down_term = contract(mixed_low, grad_branch_all, 0, 0, bf16)
    both_term = contract(normed_all, grad_both, 0, 0, bf16)
    ffn_terms = jnp.concatenate(
        [
            both_term.reshape(teams, team_rows, 2 * wide),
            jnp.pad(
                down_term.reshape(teams, down_wide, model),
                ((0, 0), (0, team_rows - down_wide), (0, 0)),
            ),
        ],
        axis=2,
    ).reshape(teams * team_rows, -1)
    ffn_terms, grad_normed_ff = lax.optimization_barrier((ffn_terms, grad_normed_ff))
    ffn_sum = lax.psum_scatter(ffn_terms.reshape(teams, team_rows, -1), ("x", "z"), scatter_dimension=0, tiled=True)[0]
    down_sum = ffn_sum[:down_wide, 2 * wide :]
    down_two = jnp.concatenate(
        [
            lax.ppermute(down_sum, all_axes, [(b, a) for a, b in before]),
            lax.ppermute(down_sum, all_axes, [(b, a) for a, b in here]),
        ],
        axis=0,
    )
    down_grad = lax.dynamic_slice_in_dim(
        down_two, down_wide - down_shift * (flat % teams), down_rows, 0
    ).astype(f32)

    grad_middle_add, grad_pre_ff = pre_pull(grad_normed_ff)
    grad_middle = grad_output + grad_middle_add
    grad_attn, grad_post_attn = post_attn_pull(grad_middle)
    grad_attn_low = grad_attn.astype(bf16)
    out_term = contract(attended_low, grad_attn_low, 0, 0, bf16)
    grad_attended = contract(grad_attn_low, full_out, 1, 1, bf16)
    grad_attended = grad_attended.reshape(tok_count, heads, head_dim).transpose(1, 0, 2)
    grad_attended = grad_attended.reshape(heads * tok_count, head_dim)

    grad_prob = contract(grad_attended, value_all, 1, 1)
    shift_term = jnp.sum(prob * grad_prob, axis=-1, keepdims=True)
    grad_scores = (prob * (grad_prob - shift_term)).astype(bf16)
    grad_query = contract(grad_scores, key_all, 1, 0) * score_scale
    grad_key = contract(grad_scores, query_low, 0, 0) * score_scale
    grad_value = contract(prob_low, grad_attended, 0, 0)
    grad_key_value = jnp.concatenate([grad_key, grad_value], axis=1)
    grad_key_value = sum_ahead(
        [grad_key_value[s * tok_count : (s + 1) * tok_count] for s in range(inner)]
    )
    grad_queries = grad_query.reshape(heads, tok_count, head_dim).transpose(1, 0, 2)
    grad_query_raw, grad_key_raw, grad_query_gain, grad_key_gain = prepare_pull(
        (grad_queries, grad_key_value[:, :head_dim])
    )
    grad_qkv = jnp.concatenate(
        [
            grad_query_raw.reshape(tok_count, query_cols),
            grad_key_raw,
            grad_key_value[:, head_dim:],
        ],
        axis=1,
    ).astype(bf16)
    qkv_term = contract(normed_low, grad_qkv, 0, 0, bf16)
    grad_normed = contract(grad_qkv, full_qkv, 1, 1)
    grad_input_add, grad_in_gain = in_pull(grad_normed)
    input_grad = grad_middle + grad_input_add

    grad_gains = (
        grad_in_gain,
        grad_query_gain,
        grad_key_gain,
        grad_post_attn,
        grad_pre_ff,
        grad_post_ff,
    )
    gain_terms = jnp.concatenate(
        [item.reshape(teams, members, -1) for item in grad_gains], axis=2
    ).astype(bf16)
    gain_terms = jnp.pad(gain_terms, ((0, 0), (0, 0), (0, model - gain_terms.shape[2])))
    attn_terms = halves(
        qkv_term.reshape(teams, team_rows, qkv_cols),
        jnp.concatenate(
            [out_term.reshape(teams, members * out_rows, model), gain_terms], axis=1
        ),
    )
    attn_half = reduce_axis(attn_terms, "core", 0)
    attn_half = attn_half.reshape(lax.axis_size("x"), lax.axis_size("z"), team_rows, half)
    left = reduce_axis(attn_half[..., :half_qkv], "x", 0)
    right = reduce_axis(attn_half[..., half_qkv:], "z", 1)
    left = reduce_axis(left, "z", 0)
    right = reduce_axis(right, "x", 0)
    attn_sum = jnp.concatenate(
        [
            left.reshape(members, rows, half_qkv),
            jnp.concatenate(
                [
                    right[: members * out_rows].reshape(members, out_rows, half_out),
                    right[members * out_rows :][:, None],
                ],
                axis=1,
            ),
        ],
        axis=2,
    ).reshape(cores, inner, rows, half)
    message = jnp.concatenate(
        [
            ffn_sum[:, : 2 * wide].reshape(cores, inner, rows, 2 * wide),
            attn_sum,
        ],
        axis=3,
    ).transpose(1, 0, 2, 3)
    by_y = swap(message, "y")
    attn_sum = jnp.sum(by_y[..., 2 * wide :].astype(f32), axis=0).astype(bf16)
    message = jnp.concatenate(
        [by_y[c, :, :, : 2 * wide] for c in range(inner)] + [attn_sum], axis=2
    )
    by_core = swap(message, "core").astype(f32)
    both_grad = jnp.concatenate(
        [
            by_core[c, None, :, k * 2 * wide : (k + 1) * 2 * wide]
            for c in range(cores)
            for k in range(inner)
        ],
        axis=0,
    ).transpose(1, 0, 2)
    gate_grad = both_grad[:, :, :part].reshape(rows, members * part)
    up_grad = both_grad[:, :, wide : wide + part].reshape(rows, members * part)
    attn_sum = by_core[:, :, inner * 2 * wide :]
    attn_grad = jnp.concatenate(
        [attn_sum[c, :, :half_qkv] for c in range(cores)]
        + [attn_sum[c, :, half_qkv:] for c in range(cores)],
        axis=1,
    )
    gain_grads = []
    first = qkv_cols
    for item in gains:
        size = item.shape[0]
        gain_grads.append(attn_grad[rows - 1, first : first + size])
        first += size
    return (
        output[None],
        input_grad[None],
        *gain_grads,
        attn_grad[:, :query_cols],
        attn_grad[:, query_cols : query_cols + head_dim],
        attn_grad[:, query_cols + head_dim : qkv_cols],
        attn_grad[:out_rows, qkv_cols : qkv_cols + model],
        gate_grad,
        up_grad,
        down_grad,
    )


def solution(mesh):
    fine = Mesh(mesh.devices.reshape(4, 4, 2, 4), ("x", "z", "core", "y"))
    all_axes = ("x", "z", "core", "y")
    shard = P(all_axes)
    matrix = P(all_axes, None)
    tokens = P(("x", "z", "core"), "y", None)
    return jax.shard_map(
        local,
        mesh=fine,
        in_specs=(tokens, tokens, P(("x", "z", "core"), None)) + (shard,) * 6 + (matrix,) * 7,
        out_specs=(tokens, tokens) + (shard,) * 6 + (matrix,) * 7,
        check_vma=False,
    )
```

```python
import math

import jax
import jax.numpy as jnp
from jax import lax
from jax.sharding import Mesh
from jax.sharding import PartitionSpec as P

norm_eps = 1e-06
rope_base = 1000000.0
score_scale = 0.0625
far_below = -1e30
f32 = jnp.float32
bf16 = jnp.bfloat16


def rms_norm(values, gain):
    factor = lax.rsqrt(jnp.mean(values * values, axis=-1, keepdims=True) + norm_eps)
    return values * factor * (1.0 + gain)


def rotate(values, cosine, sine):
    half_dim = values.shape[-1] // 2
    first_half = values[..., :half_dim]
    second_half = values[..., half_dim:]
    return jnp.concatenate(
        [first_half * cosine - second_half * sine, second_half * cosine + first_half * sine],
        axis=-1,
    )


def rope_tables(positions, head_dim):
    freq_index = jnp.arange(head_dim // 2, dtype=f32)
    inverse = jnp.exp(freq_index * (-2.0 / head_dim) * math.log(rope_base))
    angles = positions.astype(f32)[:, None] * inverse[None, :]
    return (jnp.cos(angles), jnp.sin(angles))


def gated_unit(gate_pre, up_pre):
    return jax.nn.gelu(gate_pre, approximate=True) * up_pre


def contract(left, right, left_dim, right_dim, kind=f32):
    return lax.dot_general(
        left, right, (((left_dim,), (right_dim,)), ((), ())), preferred_element_type=kind
    )


def from_ahead(block, step, axis="y"):
    size = lax.axis_size(axis)
    return lax.ppermute(block, axis, [(i, (i - step) % size) for i in range(size)])


def to_ahead(block, step, axis="y"):
    size = lax.axis_size(axis)
    return lax.ppermute(block, axis, [(i, (i + step) % size) for i in range(size)])


def gather_ahead(block, axis="y"):
    size = lax.axis_size(axis)
    return jnp.concatenate([block] + [from_ahead(block, s, axis) for s in range(1, size)], axis=0)


def sum_ahead(terms, axis="y"):
    arrived = [to_ahead(terms[s].astype(bf16), s, axis) for s in range(1, len(terms))]
    total = terms[0].astype(f32)
    for item in arrived:
        total = total + item.astype(f32)
    return total


def swap(pieces, axis):
    size = lax.axis_size(axis)
    me = lax.axis_index(axis)
    arrived = [lax.dynamic_index_in_dim(pieces, me, 0, keepdims=False)]
    for s in range(1, size):
        item = lax.dynamic_index_in_dim(pieces, (me + s) % size, 0, keepdims=False)
        arrived.append(to_ahead(item, s, axis))
    return by_sender(arrived, axis)


def by_sender(arrived, axis):
    size = lax.axis_size(axis)
    me = lax.axis_index(axis)
    result = []
    for c in range(size):
        item = arrived[0]
        for s in range(1, size):
            item = jnp.where((me - c) % size == s, arrived[s], item)
        result.append(item)
    return jnp.stack(result)


def gather_axis(block, axis, dim):
    size = lax.axis_size(axis)
    me = lax.axis_index(axis)
    arrived = [block] + [to_ahead(block, s, axis) for s in range(1, size)]
    result = jnp.zeros(block.shape[:dim] + (size,) + block.shape[dim:], block.dtype)
    for s in range(size):
        item = jnp.expand_dims(arrived[s], dim)
        result = lax.dynamic_update_slice_in_dim(result, item, (me - s) % size, dim)
    return result


def reduce_axis(terms, axis, dim):
    size = lax.axis_size(axis)
    me = lax.axis_index(axis)
    total = lax.dynamic_index_in_dim(terms, me, dim, keepdims=False).astype(f32)
    arrived = [
        to_ahead(lax.dynamic_index_in_dim(terms, (me + s) % size, dim, keepdims=False), s, axis)
        for s in range(1, size)
    ]
    for item in arrived:
        total = total + item.astype(f32)
    return total.astype(bf16)


def side_by_side(items, width):
    total, first = None, 0
    for item in items:
        last = width - first - item.shape[-1]
        placed = jnp.pad(item, ((0, 0),) * (item.ndim - 1) + ((first, last),))
        total = placed if total is None else total + placed
        first += item.shape[-1]
    return total


def gather_blocks(block, axis):
    size = lax.axis_size(axis)
    return by_sender([block] + [to_ahead(block, s, axis) for s in range(1, size)], axis)


def gather_team(block):
    return gather_ahead(gather_ahead(block, "y"), "core")


def sum_team(term, tokens):
    half = term.shape[0] // 2
    term = sum_ahead([term[:half], term[half:]], "core")
    return sum_ahead([term[i : i + tokens] for i in range(0, half, tokens)], "y")


def down_routes(teams, members):
    here, before = [], []
    for member in range(members):
        for block in range(teams):
            owner = member * teams + block
            here.append((owner, block * members + member))
            if block > 0:
                before.append((owner, (block - 1) * members + member))
    return here, before


def local(
    activations,
    cotangent,
    segments,
    in_gain,
    query_gain,
    key_gain,
    post_attn_gain,
    pre_ff_gain,
    post_ff_gain,
    w_query,
    w_key,
    w_value,
    w_out,
    w_gate,
    w_up,
    w_down,
):
    all_axes = ("x", "z", "core", "y")
    teams = lax.axis_size("x") * lax.axis_size("z")
    inner = lax.axis_size("y")
    cores = lax.axis_size("core")
    members = inner * cores
    me = lax.axis_index("y")
    team = lax.axis_index("x") * lax.axis_size("z") + lax.axis_index("z")
    flat = team * members + lax.axis_index("core") * inner + me
    rows = w_query.shape[0]
    model = w_down.shape[1]
    query_cols = w_query.shape[1]
    head_dim = w_key.shape[1]
    heads = query_cols // head_dim
    qkv_cols = query_cols + 2 * head_dim
    out_rows = w_out.shape[0]
    team_rows = members * rows
    part = w_gate.shape[1] // members
    wide = -(-part // 128) * 128
    down_rows = w_down.shape[0]
    down_wide = wide // teams
    down_shift = down_wide - down_rows

    half_qkv = qkv_cols // 2
    half_out = -(-model // 256) * 128
    half = half_qkv + half_out

    def halves(qkv_block, out_block):
        out_block = jnp.pad(out_block, ((0, 0),) * (out_block.ndim - 1) + ((0, 2 * half_out - model),))
        return jnp.stack(
            [
                jnp.concatenate(
                    [
                        qkv_block[..., c * half_qkv : (c + 1) * half_qkv],
                        out_block[..., c * half_out : (c + 1) * half_out],
                    ],
                    axis=-1,
                )
                for c in range(cores)
            ]
        )

    gains = (in_gain, query_gain, key_gain, post_attn_gain, pre_ff_gain, post_ff_gain)
    gain_row = side_by_side(gains, model)[None]
    attn_rows = halves(
        jnp.concatenate([w_query, w_key, w_value], axis=1),
        jnp.concatenate([w_out, gain_row], axis=0),
    )
    attn_rows = gather_blocks(attn_rows, "y").transpose(1, 0, 2, 3)
    attn_rows = swap(attn_rows, "core").reshape(members, rows, half)
    attn_shard = jnp.concatenate(
        [
            attn_rows[:, :, :half_qkv].reshape(team_rows, half_qkv),
            jnp.concatenate(
                [
                    attn_rows[:, :out_rows, half_qkv:].reshape(members * out_rows, half_out),
                    attn_rows[:, out_rows, half_qkv:],
                ],
                axis=0,
            ),
        ],
        axis=1,
    )
    def columns(weight):
        pieces = weight.reshape(rows, members, part)
        return jnp.pad(pieces, ((0, 0), (0, 0), (0, wide - part)))

    both = jnp.concatenate([columns(w_gate), columns(w_up)], axis=2).transpose(1, 0, 2)
    both = both.reshape(cores, inner, rows, 2 * wide)
    by_y = swap(both.transpose(1, 2, 0, 3).reshape(inner, rows, cores * 2 * wide), "y")
    by_core = by_y.reshape(inner, rows, cores, 2 * wide).transpose(2, 0, 1, 3)
    by_member = swap(by_core, "core").reshape(team_rows, 2 * wide)
    here, before = down_routes(teams, members)
    down_two = jnp.concatenate(
        [lax.ppermute(w_down, all_axes, here), lax.ppermute(w_down, all_axes, before)], axis=0
    )
    down_part = lax.dynamic_slice_in_dim(down_two, down_shift * team, down_wide, 0)
    shard = jnp.concatenate(
        [by_member, jnp.pad(down_part, ((0, team_rows - down_wide), (0, 0)))],
        axis=1,
    )
    full = lax.all_gather(shard, ("x", "z"), axis=0, tiled=True)
    attn_shard, _ = lax.optimization_barrier((attn_shard, shard))
    full_both = full[:, : 2 * wide]
    full_down = full.reshape(teams, team_rows, -1)[:, :down_wide, 2 * wide :].reshape(wide, model)

    left = gather_axis(gather_axis(attn_shard[:, :half_qkv], "x", 0), "z", 1)
    right = gather_axis(gather_axis(attn_shard[:, half_qkv:], "z", 0), "x", 0)
    left = by_sender([left, to_ahead(left, 1, "core")], "core")
    right = by_sender([right, to_ahead(right, 1, "core")], "core")
    right = right.reshape(cores, teams, team_rows, half_out)
    full_qkv = jnp.concatenate(
        [left[c].reshape(model, half_qkv) for c in range(cores)], axis=1
    )
    full_out = jnp.concatenate(
        [
            right[c, :, : members * out_rows].reshape(query_cols, half_out)
            for c in range(cores)
        ],
        axis=1,
    )[:, :model]
    gain_all = right[0, :, members * out_rows :, :128].astype(f32)
    full_gains = []
    first = 0
    for item in gains:
        size = item.shape[0]
        full_gains.append(gain_all[:, :, first : first + size].reshape(-1))
        first += size
    gain_in, gain_query, gain_key, gain_post_attn, gain_pre, gain_post = full_gains

    inputs = activations[0].astype(f32)
    segment_all = segments[0]
    tok_count = inputs.shape[0]
    first_place = me * tok_count
    place_rows = first_place + jnp.arange(tok_count, dtype=jnp.int32)
    segment_rows = lax.dynamic_slice_in_dim(segment_all, first_place, tok_count)
    earlier = jnp.sum((segment_all[None, :] < segment_rows[:, None]).astype(jnp.int32), axis=1)
    cosine, sine = rope_tables(place_rows - earlier, head_dim)
    length = segment_all.shape[0]
    key_places = (first_place + jnp.arange(length, dtype=jnp.int32)) % length
    key_segments = lax.dynamic_slice_in_dim(
        jnp.concatenate([segment_all, segment_all]), first_place, length
    )
    allowed = (segment_rows[:, None] == key_segments[None, :]) & (
        place_rows[:, None] >= key_places[None, :]
    )
    allowed = jnp.tile(allowed, (heads, 1))

    normed, in_pull = jax.vjp(rms_norm, inputs, gain_in)
    normed_low = normed.astype(bf16)
    qkv = contract(normed_low, full_qkv, 1, 0)
    query_raw = qkv[:, :query_cols].reshape(tok_count, heads, head_dim)
    key_raw = qkv[:, query_cols : query_cols + head_dim]
    value_low = qkv[:, query_cols + head_dim :].astype(bf16)

    def prepare(query_in, key_in, query_scale, key_scale):
        rotated_query = rotate(
            rms_norm(query_in, query_scale), cosine[:, None, :], sine[:, None, :]
        )
        rotated_key = rotate(rms_norm(key_in, key_scale), cosine, sine)
        return (rotated_query, rotated_key)

    (queries, key_rows), prepare_pull = jax.vjp(prepare, query_raw, key_raw, gain_query, gain_key)
    query_low = queries.astype(bf16).transpose(1, 0, 2).reshape(heads * tok_count, head_dim)
    key_value = gather_ahead(jnp.concatenate([key_rows.astype(bf16), value_low], axis=1))
    key_all = key_value[:, :head_dim]
    value_all = key_value[:, head_dim:]

    scores = contract(query_low, key_all, 1, 1) * score_scale
    scores = jnp.where(allowed, scores, far_below)
    top_score = jnp.max(scores, axis=-1, keepdims=True)
    weight = jnp.exp(scores - top_score)
    prob = weight / jnp.sum(weight, axis=-1, keepdims=True)
    prob_low = prob.astype(bf16)
    attended = contract(prob_low, value_all, 1, 0).astype(bf16)
    attended_low = attended.reshape(heads, tok_count, head_dim).transpose(1, 0, 2)
    attended_low = attended_low.reshape(tok_count, query_cols)
    attn_out = contract(attended_low, full_out, 1, 0)
    post_attn, post_attn_pull = jax.vjp(rms_norm, attn_out, gain_post_attn)
    middle = inputs + post_attn
    normed_ff, pre_pull = jax.vjp(rms_norm, middle, gain_pre)
    normed_all = gather_team(normed_ff.astype(bf16))

    gate_up = contract(normed_all, full_both, 1, 0)
    mixed, gated_pull = jax.vjp(gated_unit, gate_up[:, :wide], gate_up[:, wide:])
    mixed_low = mixed.astype(bf16)
    team_half = inner * tok_count
    branch_other = to_ahead(contract(mixed_low[team_half:], full_down, 1, 0, bf16), 1, "core")
    branch_term = contract(mixed_low[:team_half], full_down, 1, 0) + branch_other.astype(f32)
    branch_out = sum_ahead(
        [branch_term[i : i + tok_count] for i in range(0, team_half, tok_count)], "y"
    )
    post_ff, post_pull = jax.vjp(rms_norm, branch_out, gain_post)
    output = (middle + post_ff).astype(bf16)

    grad_output = cotangent[0].astype(f32)
    grad_branch, grad_post_ff = post_pull(grad_output)
    grad_branch_all = gather_team(grad_branch.astype(bf16))
    grad_mixed = contract(grad_branch_all, full_down, 1, 1)
    grad_gate, grad_up = gated_pull(grad_mixed)
    grad_both = jnp.concatenate([grad_gate.astype(bf16), grad_up.astype(bf16)], axis=1)
    grad_normed_term = contract(grad_both, full_both, 1, 1)
    grad_both, mixed_low, grad_normed_term = lax.optimization_barrier(
        (grad_both, mixed_low, grad_normed_term)
    )
    grad_normed_ff = sum_team(grad_normed_term, tok_count)
    down_term = contract(mixed_low, grad_branch_all, 0, 0, bf16)
    both_term = contract(normed_all, grad_both, 0, 0, bf16)
    ffn_terms = jnp.concatenate(
        [
            both_term.reshape(teams, team_rows, 2 * wide),
            jnp.pad(
                down_term.reshape(teams, down_wide, model),
                ((0, 0), (0, team_rows - down_wide), (0, 0)),
            ),
        ],
        axis=2,
    ).reshape(teams * team_rows, -1)
    grad_normed_ff, _ = lax.optimization_barrier((grad_normed_ff, ffn_terms))
    ffn_sum = lax.psum_scatter(ffn_terms.reshape(teams, team_rows, -1), ("x", "z"), scatter_dimension=0, tiled=True)[0]
    down_sum = ffn_sum[:down_wide, 2 * wide :]
    down_two = jnp.concatenate(
        [
            lax.ppermute(down_sum, all_axes, [(b, a) for a, b in before]),
            lax.ppermute(down_sum, all_axes, [(b, a) for a, b in here]),
        ],
        axis=0,
    )
    down_grad = lax.dynamic_slice_in_dim(
        down_two, down_wide - down_shift * (flat % teams), down_rows, 0
    ).astype(f32)

    grad_middle_add, grad_pre_ff = pre_pull(grad_normed_ff)
    grad_middle = grad_output + grad_middle_add
    grad_attn, grad_post_attn = post_attn_pull(grad_middle)
    grad_attn_low = grad_attn.astype(bf16)
    out_term = contract(attended_low, grad_attn_low, 0, 0, bf16)
    grad_attended = contract(grad_attn_low, full_out, 1, 1, bf16)
    grad_attended = grad_attended.reshape(tok_count, heads, head_dim).transpose(1, 0, 2)
    grad_attended = grad_attended.reshape(heads * tok_count, head_dim)

    grad_prob = contract(grad_attended, value_all, 1, 1)
    shift_term = jnp.sum(prob * grad_prob, axis=-1, keepdims=True)
    grad_scores = (prob * (grad_prob - shift_term)).astype(bf16)
    grad_query = contract(grad_scores, key_all, 1, 0) * score_scale
    grad_key = contract(grad_scores, query_low, 0, 0) * score_scale
    grad_value = contract(prob_low, grad_attended, 0, 0)
    grad_key_value = jnp.concatenate([grad_key, grad_value], axis=1)
    grad_key_value = sum_ahead(
        [grad_key_value[s * tok_count : (s + 1) * tok_count] for s in range(inner)]
    )
    grad_queries = grad_query.reshape(heads, tok_count, head_dim).transpose(1, 0, 2)
    grad_query_raw, grad_key_raw, grad_query_gain, grad_key_gain = prepare_pull(
        (grad_queries, grad_key_value[:, :head_dim])
    )
    grad_qkv = jnp.concatenate(
        [
            grad_query_raw.reshape(tok_count, query_cols),
            grad_key_raw,
            grad_key_value[:, head_dim:],
        ],
        axis=1,
    ).astype(bf16)
    qkv_term = contract(normed_low, grad_qkv, 0, 0, bf16)
    grad_normed = contract(grad_qkv, full_qkv, 1, 1)
    grad_input_add, grad_in_gain = in_pull(grad_normed)
    input_grad = grad_middle + grad_input_add

    grad_gains = (
        grad_in_gain,
        grad_query_gain,
        grad_key_gain,
        grad_post_attn,
        grad_pre_ff,
        grad_post_ff,
    )
    gain_terms = jnp.concatenate(
        [item.reshape(teams, members, -1) for item in grad_gains], axis=2
    ).astype(bf16)
    gain_terms = jnp.pad(gain_terms, ((0, 0), (0, 0), (0, model - gain_terms.shape[2])))
    attn_terms = halves(
        qkv_term.reshape(teams, team_rows, qkv_cols),
        jnp.concatenate(
            [out_term.reshape(teams, members * out_rows, model), gain_terms], axis=1
        ),
    )
    attn_half = reduce_axis(attn_terms, "core", 0)
    attn_half = attn_half.reshape(lax.axis_size("x"), lax.axis_size("z"), team_rows, half)
    left = reduce_axis(attn_half[..., :half_qkv], "x", 0)
    right = reduce_axis(attn_half[..., half_qkv:], "z", 1)
    left = reduce_axis(left, "z", 0)
    right = reduce_axis(right, "x", 0)
    attn_sum = jnp.concatenate(
        [
            left.reshape(members, rows, half_qkv),
            jnp.concatenate(
                [
                    right[: members * out_rows].reshape(members, out_rows, half_out),
                    right[members * out_rows :][:, None],
                ],
                axis=1,
            ),
        ],
        axis=2,
    ).reshape(cores, inner, rows, half)
    message = jnp.concatenate(
        [
            ffn_sum[:, : 2 * wide].reshape(cores, inner, rows, 2 * wide),
            attn_sum,
        ],
        axis=3,
    ).transpose(1, 0, 2, 3)
    by_y = swap(message, "y")
    attn_sum = jnp.sum(by_y[..., 2 * wide :].astype(f32), axis=0).astype(bf16)
    message = jnp.concatenate(
        [by_y[c, :, :, : 2 * wide] for c in range(inner)] + [attn_sum], axis=2
    )
    by_core = swap(message, "core").astype(f32)
    both_grad = jnp.concatenate(
        [
            by_core[c, None, :, k * 2 * wide : (k + 1) * 2 * wide]
            for c in range(cores)
            for k in range(inner)
        ],
        axis=0,
    ).transpose(1, 0, 2)
    gate_grad = both_grad[:, :, :part].reshape(rows, members * part)
    up_grad = both_grad[:, :, wide : wide + part].reshape(rows, members * part)
    attn_sum = by_core[:, :, inner * 2 * wide :]
    attn_grad = jnp.concatenate(
        [attn_sum[c, :, :half_qkv] for c in range(cores)]
        + [attn_sum[c, :, half_qkv:] for c in range(cores)],
        axis=1,
    )
    gain_grads = []
    first = qkv_cols
    for item in gains:
        size = item.shape[0]
        gain_grads.append(attn_grad[rows - 1, first : first + size])
        first += size
    return (
        output[None],
        input_grad[None],
        *gain_grads,
        attn_grad[:, :query_cols],
        attn_grad[:, query_cols : query_cols + head_dim],
        attn_grad[:, query_cols + head_dim : qkv_cols],
        attn_grad[:out_rows, qkv_cols : qkv_cols + model],
        gate_grad,
        up_grad,
        down_grad,
    )


def solution(mesh):
    fine = Mesh(mesh.devices.reshape(4, 4, 2, 4), ("x", "z", "core", "y"))
    all_axes = ("x", "z", "core", "y")
    shard = P(all_axes)
    matrix = P(all_axes, None)
    tokens = P(("x", "z", "core"), "y", None)
    return jax.shard_map(
        local,
        mesh=fine,
        in_specs=(tokens, tokens, P(("x", "z", "core"), None)) + (shard,) * 6 + (matrix,) * 7,
        out_specs=(tokens, tokens) + (shard,) * 6 + (matrix,) * 7,
        check_vma=False,
    )
```

```python
import math

import jax
import jax.numpy as jnp
from jax import lax
from jax.sharding import Mesh
from jax.sharding import PartitionSpec as P

norm_eps = 1e-06
rope_base = 1000000.0
score_scale = 0.0625
far_below = -1e30
f32 = jnp.float32
bf16 = jnp.bfloat16


def rms_norm(values, gain):
    factor = lax.rsqrt(jnp.mean(values * values, axis=-1, keepdims=True) + norm_eps)
    return values * factor * (1.0 + gain)


def rotate(values, cosine, sine):
    half_dim = values.shape[-1] // 2
    first_half = values[..., :half_dim]
    second_half = values[..., half_dim:]
    return jnp.concatenate(
        [first_half * cosine - second_half * sine, second_half * cosine + first_half * sine],
        axis=-1,
    )


def rope_tables(positions, head_dim):
    freq_index = jnp.arange(head_dim // 2, dtype=f32)
    inverse = jnp.exp(freq_index * (-2.0 / head_dim) * math.log(rope_base))
    angles = positions.astype(f32)[:, None] * inverse[None, :]
    return (jnp.cos(angles), jnp.sin(angles))


def gated_unit(gate_pre, up_pre):
    return jax.nn.gelu(gate_pre, approximate=True) * up_pre


def contract(left, right, left_dim, right_dim, kind=f32):
    return lax.dot_general(
        left, right, (((left_dim,), (right_dim,)), ((), ())), preferred_element_type=kind
    )


def from_ahead(block, step, axis="y"):
    size = lax.axis_size(axis)
    return lax.ppermute(block, axis, [(i, (i - step) % size) for i in range(size)])


def to_ahead(block, step, axis="y"):
    size = lax.axis_size(axis)
    return lax.ppermute(block, axis, [(i, (i + step) % size) for i in range(size)])


def gather_ahead(block, axis="y"):
    size = lax.axis_size(axis)
    return jnp.concatenate([block] + [from_ahead(block, s, axis) for s in range(1, size)], axis=0)


def sum_ahead(terms, axis="y"):
    arrived = [to_ahead(terms[s].astype(bf16), s, axis) for s in range(1, len(terms))]
    total = terms[0].astype(f32)
    for item in arrived:
        total = total + item.astype(f32)
    return total


def swap(pieces, axis):
    size = lax.axis_size(axis)
    me = lax.axis_index(axis)
    arrived = [lax.dynamic_index_in_dim(pieces, me, 0, keepdims=False)]
    for s in range(1, size):
        item = lax.dynamic_index_in_dim(pieces, (me + s) % size, 0, keepdims=False)
        arrived.append(to_ahead(item, s, axis))
    return by_sender(arrived, axis)


def by_sender(arrived, axis):
    size = lax.axis_size(axis)
    me = lax.axis_index(axis)
    result = []
    for c in range(size):
        item = arrived[0]
        for s in range(1, size):
            item = jnp.where((me - c) % size == s, arrived[s], item)
        result.append(item)
    return jnp.stack(result)


def gather_axis(block, axis, dim):
    size = lax.axis_size(axis)
    me = lax.axis_index(axis)
    arrived = [block] + [to_ahead(block, s, axis) for s in range(1, size)]
    result = jnp.zeros(block.shape[:dim] + (size,) + block.shape[dim:], block.dtype)
    for s in range(size):
        item = jnp.expand_dims(arrived[s], dim)
        result = lax.dynamic_update_slice_in_dim(result, item, (me - s) % size, dim)
    return result


def reduce_axis(terms, axis, dim):
    size = lax.axis_size(axis)
    me = lax.axis_index(axis)
    total = lax.dynamic_index_in_dim(terms, me, dim, keepdims=False).astype(f32)
    arrived = [
        to_ahead(lax.dynamic_index_in_dim(terms, (me + s) % size, dim, keepdims=False), s, axis)
        for s in range(1, size)
    ]
    for item in arrived:
        total = total + item.astype(f32)
    return total.astype(bf16)


def side_by_side(items, width):
    total, first = None, 0
    for item in items:
        last = width - first - item.shape[-1]
        placed = jnp.pad(item, ((0, 0),) * (item.ndim - 1) + ((first, last),))
        total = placed if total is None else total + placed
        first += item.shape[-1]
    return total


def gather_blocks(block, axis):
    size = lax.axis_size(axis)
    return by_sender([block] + [to_ahead(block, s, axis) for s in range(1, size)], axis)


def gather_team(block):
    return gather_ahead(gather_ahead(block, "y"), "core")


def sum_team(term, tokens):
    half = term.shape[0] // 2
    term = sum_ahead([term[:half], term[half:]], "core")
    return sum_ahead([term[i : i + tokens] for i in range(0, half, tokens)], "y")


def down_routes(teams, members):
    here, before = [], []
    for member in range(members):
        for block in range(teams):
            owner = member * teams + block
            here.append((owner, block * members + member))
            if block > 0:
                before.append((owner, (block - 1) * members + member))
    return here, before


def local(
    activations,
    cotangent,
    segments,
    in_gain,
    query_gain,
    key_gain,
    post_attn_gain,
    pre_ff_gain,
    post_ff_gain,
    w_query,
    w_key,
    w_value,
    w_out,
    w_gate,
    w_up,
    w_down,
):
    all_axes = ("x", "z", "core", "y")
    teams = lax.axis_size("x") * lax.axis_size("z")
    inner = lax.axis_size("y")
    cores = lax.axis_size("core")
    members = inner * cores
    me = lax.axis_index("y")
    team = lax.axis_index("x") * lax.axis_size("z") + lax.axis_index("z")
    flat = team * members + lax.axis_index("core") * inner + me
    rows = w_query.shape[0]
    model = w_down.shape[1]
    query_cols = w_query.shape[1]
    head_dim = w_key.shape[1]
    heads = query_cols // head_dim
    qkv_cols = query_cols + 2 * head_dim
    out_rows = w_out.shape[0]
    team_rows = members * rows
    part = w_gate.shape[1] // members
    wide = -(-part // 128) * 128
    down_rows = w_down.shape[0]
    down_wide = wide // teams
    down_shift = down_wide - down_rows

    half_qkv = qkv_cols // 2
    half_out = -(-model // 256) * 128
    half = half_qkv + half_out

    def halves(qkv_block, out_block):
        out_block = jnp.pad(out_block, ((0, 0),) * (out_block.ndim - 1) + ((0, 2 * half_out - model),))
        return jnp.stack(
            [
                jnp.concatenate(
                    [
                        qkv_block[..., c * half_qkv : (c + 1) * half_qkv],
                        out_block[..., c * half_out : (c + 1) * half_out],
                    ],
                    axis=-1,
                )
                for c in range(cores)
            ]
        )

    gains = (in_gain, query_gain, key_gain, post_attn_gain, pre_ff_gain, post_ff_gain)
    gain_row = side_by_side(gains, model)[None]
    attn_rows = halves(
        jnp.concatenate([w_query, w_key, w_value], axis=1),
        jnp.concatenate([w_out, gain_row], axis=0),
    )
    attn_rows = gather_blocks(attn_rows, "y").transpose(1, 0, 2, 3)
    attn_rows, w_down = lax.optimization_barrier((attn_rows, w_down))
    attn_rows = swap(attn_rows, "core").reshape(members, rows, half)
    attn_shard = jnp.concatenate(
        [
            attn_rows[:, :, :half_qkv].reshape(team_rows, half_qkv),
            jnp.concatenate(
                [
                    attn_rows[:, :out_rows, half_qkv:].reshape(members * out_rows, half_out),
                    attn_rows[:, out_rows, half_qkv:],
                ],
                axis=0,
            ),
        ],
        axis=1,
    )
    def columns(weight):
        pieces = weight.reshape(rows, members, part)
        return jnp.pad(pieces, ((0, 0), (0, 0), (0, wide - part)))

    both = jnp.concatenate([columns(w_gate), columns(w_up)], axis=2).transpose(1, 0, 2)
    both = both.reshape(cores, inner, rows, 2 * wide)
    by_y = swap(both.transpose(1, 2, 0, 3).reshape(inner, rows, cores * 2 * wide), "y")
    by_core = by_y.reshape(inner, rows, cores, 2 * wide).transpose(2, 0, 1, 3)
    by_member = swap(by_core, "core").reshape(team_rows, 2 * wide)
    here, before = down_routes(teams, members)
    down_two = jnp.concatenate(
        [lax.ppermute(w_down, all_axes, here), lax.ppermute(w_down, all_axes, before)], axis=0
    )
    down_part = lax.dynamic_slice_in_dim(down_two, down_shift * team, down_wide, 0)
    shard = jnp.concatenate(
        [by_member, jnp.pad(down_part, ((0, team_rows - down_wide), (0, 0)))],
        axis=1,
    )
    full = lax.all_gather(shard, ("x", "z"), axis=0, tiled=True)
    full_both = full[:, : 2 * wide]
    full_down = full.reshape(teams, team_rows, -1)[:, :down_wide, 2 * wide :].reshape(wide, model)

    left = gather_axis(attn_shard[:, :half_qkv], "x", 0)
    right = gather_axis(attn_shard[:, half_qkv:], "z", 0)
    left, right, _ = lax.optimization_barrier((left, right, shard))
    left = gather_axis(left, "z", 1)
    right = gather_axis(right, "x", 0)
    left = by_sender([left, to_ahead(left, 1, "core")], "core")
    right = by_sender([right, to_ahead(right, 1, "core")], "core")
    right = right.reshape(cores, teams, team_rows, half_out)
    full_qkv = jnp.concatenate(
        [left[c].reshape(model, half_qkv) for c in range(cores)], axis=1
    )
    full_out = jnp.concatenate(
        [
            right[c, :, : members * out_rows].reshape(query_cols, half_out)
            for c in range(cores)
        ],
        axis=1,
    )[:, :model]
    gain_all = right[0, :, members * out_rows :, :128].astype(f32)
    full_gains = []
    first = 0
    for item in gains:
        size = item.shape[0]
        full_gains.append(gain_all[:, :, first : first + size].reshape(-1))
        first += size
    gain_in, gain_query, gain_key, gain_post_attn, gain_pre, gain_post = full_gains

    inputs = activations[0].astype(f32)
    segment_all = segments[0]
    tok_count = inputs.shape[0]
    first_place = me * tok_count
    place_rows = first_place + jnp.arange(tok_count, dtype=jnp.int32)
    segment_rows = lax.dynamic_slice_in_dim(segment_all, first_place, tok_count)
    earlier = jnp.sum((segment_all[None, :] < segment_rows[:, None]).astype(jnp.int32), axis=1)
    cosine, sine = rope_tables(place_rows - earlier, head_dim)
    length = segment_all.shape[0]
    key_places = (first_place + jnp.arange(length, dtype=jnp.int32)) % length
    key_segments = lax.dynamic_slice_in_dim(
        jnp.concatenate([segment_all, segment_all]), first_place, length
    )
    allowed = (segment_rows[:, None] == key_segments[None, :]) & (
        place_rows[:, None] >= key_places[None, :]
    )
    allowed = jnp.tile(allowed, (heads, 1))

    normed, in_pull = jax.vjp(rms_norm, inputs, gain_in)
    normed_low = normed.astype(bf16)
    qkv = contract(normed_low, full_qkv, 1, 0)
    query_raw = qkv[:, :query_cols].reshape(tok_count, heads, head_dim)
    key_raw = qkv[:, query_cols : query_cols + head_dim]
    value_low = qkv[:, query_cols + head_dim :].astype(bf16)

    def prepare(query_in, key_in, query_scale, key_scale):
        rotated_query = rotate(
            rms_norm(query_in, query_scale), cosine[:, None, :], sine[:, None, :]
        )
        rotated_key = rotate(rms_norm(key_in, key_scale), cosine, sine)
        return (rotated_query, rotated_key)

    (queries, key_rows), prepare_pull = jax.vjp(prepare, query_raw, key_raw, gain_query, gain_key)
    query_low = queries.astype(bf16).transpose(1, 0, 2).reshape(heads * tok_count, head_dim)
    key_value = gather_ahead(jnp.concatenate([key_rows.astype(bf16), value_low], axis=1))
    key_all = key_value[:, :head_dim]
    value_all = key_value[:, head_dim:]

    scores = contract(query_low, key_all, 1, 1) * score_scale
    scores = jnp.where(allowed, scores, far_below)
    top_score = jnp.max(scores, axis=-1, keepdims=True)
    weight = jnp.exp(scores - top_score)
    prob = weight / jnp.sum(weight, axis=-1, keepdims=True)
    prob_low = prob.astype(bf16)
    attended = contract(prob_low, value_all, 1, 0).astype(bf16)
    attended_low = attended.reshape(heads, tok_count, head_dim).transpose(1, 0, 2)
    attended_low = attended_low.reshape(tok_count, query_cols)
    attn_out = contract(attended_low, full_out, 1, 0)
    post_attn, post_attn_pull = jax.vjp(rms_norm, attn_out, gain_post_attn)
    middle = inputs + post_attn
    normed_ff, pre_pull = jax.vjp(rms_norm, middle, gain_pre)
    normed_all = gather_team(normed_ff.astype(bf16))

    gate_up = contract(normed_all, full_both, 1, 0)
    mixed, gated_pull = jax.vjp(gated_unit, gate_up[:, :wide], gate_up[:, wide:])
    mixed_low = mixed.astype(bf16)
    team_half = inner * tok_count
    branch_other = to_ahead(contract(mixed_low[team_half:], full_down, 1, 0, bf16), 1, "core")
    branch_term = contract(mixed_low[:team_half], full_down, 1, 0) + branch_other.astype(f32)
    branch_out = sum_ahead(
        [branch_term[i : i + tok_count] for i in range(0, team_half, tok_count)], "y"
    )
    post_ff, post_pull = jax.vjp(rms_norm, branch_out, gain_post)
    output = (middle + post_ff).astype(bf16)

    grad_output = cotangent[0].astype(f32)
    grad_branch, grad_post_ff = post_pull(grad_output)
    grad_branch_all = gather_team(grad_branch.astype(bf16))
    grad_mixed = contract(grad_branch_all, full_down, 1, 1)
    grad_gate, grad_up = gated_pull(grad_mixed)
    grad_both = jnp.concatenate([grad_gate.astype(bf16), grad_up.astype(bf16)], axis=1)
    grad_normed_term = contract(grad_both, full_both, 1, 1)
    grad_both, mixed_low, grad_normed_term = lax.optimization_barrier(
        (grad_both, mixed_low, grad_normed_term)
    )
    grad_normed_ff = sum_team(grad_normed_term, tok_count)
    down_term = contract(mixed_low, grad_branch_all, 0, 0, bf16)
    both_term = contract(normed_all, grad_both, 0, 0, bf16)
    ffn_terms = jnp.concatenate(
        [
            both_term.reshape(teams, team_rows, 2 * wide),
            jnp.pad(
                down_term.reshape(teams, down_wide, model),
                ((0, 0), (0, team_rows - down_wide), (0, 0)),
            ),
        ],
        axis=2,
    ).reshape(teams * team_rows, -1)
    grad_normed_ff, _ = lax.optimization_barrier((grad_normed_ff, ffn_terms))
    ffn_sum = lax.psum_scatter(ffn_terms.reshape(teams, team_rows, -1), ("x", "z"), scatter_dimension=0, tiled=True)[0]

    grad_middle_add, grad_pre_ff = pre_pull(grad_normed_ff)
    grad_middle = grad_output + grad_middle_add
    grad_attn, grad_post_attn = post_attn_pull(grad_middle)
    grad_attn_low = grad_attn.astype(bf16)
    out_term = contract(attended_low, grad_attn_low, 0, 0, bf16)
    grad_attended = contract(grad_attn_low, full_out, 1, 1, bf16)
    grad_attended = grad_attended.reshape(tok_count, heads, head_dim).transpose(1, 0, 2)
    grad_attended = grad_attended.reshape(heads * tok_count, head_dim)

    grad_prob = contract(grad_attended, value_all, 1, 1)
    shift_term = jnp.sum(prob * grad_prob, axis=-1, keepdims=True)
    grad_scores = (prob * (grad_prob - shift_term)).astype(bf16)
    grad_query = contract(grad_scores, key_all, 1, 0) * score_scale
    grad_key = contract(grad_scores, query_low, 0, 0) * score_scale
    grad_value = contract(prob_low, grad_attended, 0, 0)
    grad_key_value = jnp.concatenate([grad_key, grad_value], axis=1)
    grad_key_value = sum_ahead(
        [grad_key_value[s * tok_count : (s + 1) * tok_count] for s in range(inner)]
    )
    grad_queries = grad_query.reshape(heads, tok_count, head_dim).transpose(1, 0, 2)
    grad_query_raw, grad_key_raw, grad_query_gain, grad_key_gain = prepare_pull(
        (grad_queries, grad_key_value[:, :head_dim])
    )
    grad_qkv = jnp.concatenate(
        [
            grad_query_raw.reshape(tok_count, query_cols),
            grad_key_raw,
            grad_key_value[:, head_dim:],
        ],
        axis=1,
    ).astype(bf16)
    qkv_term = contract(normed_low, grad_qkv, 0, 0, bf16)
    grad_normed = contract(grad_qkv, full_qkv, 1, 1)
    grad_input_add, grad_in_gain = in_pull(grad_normed)
    input_grad = grad_middle + grad_input_add

    grad_gains = (
        grad_in_gain,
        grad_query_gain,
        grad_key_gain,
        grad_post_attn,
        grad_pre_ff,
        grad_post_ff,
    )
    gain_terms = jnp.concatenate(
        [item.reshape(teams, members, -1) for item in grad_gains], axis=2
    ).astype(bf16)
    gain_terms = jnp.pad(gain_terms, ((0, 0), (0, 0), (0, model - gain_terms.shape[2])))
    attn_terms = halves(
        qkv_term.reshape(teams, team_rows, qkv_cols),
        jnp.concatenate(
            [out_term.reshape(teams, members * out_rows, model), gain_terms], axis=1
        ),
    )
    attn_half = reduce_axis(attn_terms, "core", 0)
    attn_half = attn_half.reshape(lax.axis_size("x"), lax.axis_size("z"), team_rows, half)
    left = reduce_axis(attn_half[..., :half_qkv], "x", 0)
    right = reduce_axis(attn_half[..., half_qkv:], "z", 1)
    right, ffn_sum = lax.optimization_barrier((right, ffn_sum))
    left = reduce_axis(left, "z", 0)
    right = reduce_axis(right, "x", 0)
    attn_sum = jnp.concatenate(
        [
            left.reshape(members, rows, half_qkv),
            jnp.concatenate(
                [
                    right[: members * out_rows].reshape(members, out_rows, half_out),
                    right[members * out_rows :][:, None],
                ],
                axis=1,
            ),
        ],
        axis=2,
    ).reshape(cores, inner, rows, half)
    down_sum = ffn_sum[:down_wide, 2 * wide :]
    down_two = jnp.concatenate(
        [
            lax.ppermute(down_sum, all_axes, [(b, a) for a, b in before]),
            lax.ppermute(down_sum, all_axes, [(b, a) for a, b in here]),
        ],
        axis=0,
    )
    down_grad = lax.dynamic_slice_in_dim(
        down_two, down_wide - down_shift * (flat % teams), down_rows, 0
    ).astype(f32)
    attn_sum, down_grad = lax.optimization_barrier((attn_sum, down_grad))

    message = jnp.concatenate(
        [
            ffn_sum[:, : 2 * wide].reshape(cores, inner, rows, 2 * wide),
            attn_sum,
        ],
        axis=3,
    ).transpose(1, 0, 2, 3)
    by_y = swap(message, "y")
    attn_sum = jnp.sum(by_y[..., 2 * wide :].astype(f32), axis=0).astype(bf16)
    message = jnp.concatenate(
        [by_y[c, :, :, : 2 * wide] for c in range(inner)] + [attn_sum], axis=2
    )
    by_core = swap(message, "core").astype(f32)
    both_grad = jnp.concatenate(
        [
            by_core[c, None, :, k * 2 * wide : (k + 1) * 2 * wide]
            for c in range(cores)
            for k in range(inner)
        ],
        axis=0,
    ).transpose(1, 0, 2)
    gate_grad = both_grad[:, :, :part].reshape(rows, members * part)
    up_grad = both_grad[:, :, wide : wide + part].reshape(rows, members * part)
    attn_sum = by_core[:, :, inner * 2 * wide :]
    attn_grad = jnp.concatenate(
        [attn_sum[c, :, :half_qkv] for c in range(cores)]
        + [attn_sum[c, :, half_qkv:] for c in range(cores)],
        axis=1,
    )
    gain_grads = []
    first = qkv_cols
    for item in gains:
        size = item.shape[0]
        gain_grads.append(attn_grad[rows - 1, first : first + size])
        first += size
    return (
        output[None],
        input_grad[None],
        *gain_grads,
        attn_grad[:, :query_cols],
        attn_grad[:, query_cols : query_cols + head_dim],
        attn_grad[:, query_cols + head_dim : qkv_cols],
        attn_grad[:out_rows, qkv_cols : qkv_cols + model],
        gate_grad,
        up_grad,
        down_grad,
    )


def solution(mesh):
    fine = Mesh(mesh.devices.reshape(4, 4, 2, 4), ("x", "z", "core", "y"))
    all_axes = ("x", "z", "core", "y")
    shard = P(all_axes)
    matrix = P(all_axes, None)
    tokens = P(("x", "z", "core"), "y", None)
    return jax.shard_map(
        local,
        mesh=fine,
        in_specs=(tokens, tokens, P(("x", "z", "core"), None)) + (shard,) * 6 + (matrix,) * 7,
        out_specs=(tokens, tokens) + (shard,) * 6 + (matrix,) * 7,
        check_vma=False,
    )
```

```python
import math

import jax
import jax.numpy as jnp
from jax import lax
from jax.sharding import Mesh
from jax.sharding import PartitionSpec as P

norm_eps = 1e-06
rope_base = 1000000.0
score_scale = 0.0625
far_below = -1e30
f32 = jnp.float32
bf16 = jnp.bfloat16


def rms_norm(values, gain):
    factor = lax.rsqrt(jnp.mean(values * values, axis=-1, keepdims=True) + norm_eps)
    return values * factor * (1.0 + gain)


def rotate(values, cosine, sine):
    half_dim = values.shape[-1] // 2
    first_half = values[..., :half_dim]
    second_half = values[..., half_dim:]
    return jnp.concatenate(
        [first_half * cosine - second_half * sine, second_half * cosine + first_half * sine],
        axis=-1,
    )


def rope_tables(positions, head_dim):
    freq_index = jnp.arange(head_dim // 2, dtype=f32)
    inverse = jnp.exp(freq_index * (-2.0 / head_dim) * math.log(rope_base))
    angles = positions.astype(f32)[:, None] * inverse[None, :]
    return (jnp.cos(angles), jnp.sin(angles))


def gated_unit(gate_pre, up_pre):
    return jax.nn.gelu(gate_pre, approximate=True) * up_pre


def contract(left, right, left_dim, right_dim, kind=f32):
    return lax.dot_general(
        left, right, (((left_dim,), (right_dim,)), ((), ())), preferred_element_type=kind
    )


def from_ahead(block, step, axis="y"):
    size = lax.axis_size(axis)
    return lax.ppermute(block, axis, [(i, (i - step) % size) for i in range(size)])


def to_ahead(block, step, axis="y"):
    size = lax.axis_size(axis)
    return lax.ppermute(block, axis, [(i, (i + step) % size) for i in range(size)])


def gather_ahead(block, axis="y"):
    size = lax.axis_size(axis)
    return jnp.concatenate([block] + [from_ahead(block, s, axis) for s in range(1, size)], axis=0)


def sum_ahead(terms, axis="y"):
    arrived = [to_ahead(terms[s].astype(bf16), s, axis) for s in range(1, len(terms))]
    total = terms[0].astype(f32)
    for item in arrived:
        total = total + item.astype(f32)
    return total


def swap(pieces, axis):
    size = lax.axis_size(axis)
    me = lax.axis_index(axis)
    arrived = [lax.dynamic_index_in_dim(pieces, me, 0, keepdims=False)]
    for s in range(1, size):
        item = lax.dynamic_index_in_dim(pieces, (me + s) % size, 0, keepdims=False)
        arrived.append(to_ahead(item, s, axis))
    return by_sender(arrived, axis)


def by_sender(arrived, axis):
    size = lax.axis_size(axis)
    me = lax.axis_index(axis)
    result = []
    for c in range(size):
        item = arrived[0]
        for s in range(1, size):
            item = jnp.where((me - c) % size == s, arrived[s], item)
        result.append(item)
    return jnp.stack(result)


def gather_axis(block, axis, dim):
    size = lax.axis_size(axis)
    me = lax.axis_index(axis)
    arrived = [block] + [to_ahead(block, s, axis) for s in range(1, size)]
    result = jnp.zeros(block.shape[:dim] + (size,) + block.shape[dim:], block.dtype)
    for s in range(size):
        item = jnp.expand_dims(arrived[s], dim)
        result = lax.dynamic_update_slice_in_dim(result, item, (me - s) % size, dim)
    return result


def reduce_axis(terms, axis, dim):
    size = lax.axis_size(axis)
    me = lax.axis_index(axis)
    total = lax.dynamic_index_in_dim(terms, me, dim, keepdims=False).astype(f32)
    arrived = [
        to_ahead(lax.dynamic_index_in_dim(terms, (me + s) % size, dim, keepdims=False), s, axis)
        for s in range(1, size)
    ]
    for item in arrived:
        total = total + item.astype(f32)
    return total.astype(bf16)


def side_by_side(items, width):
    total, first = None, 0
    for item in items:
        last = width - first - item.shape[-1]
        placed = jnp.pad(item, ((0, 0),) * (item.ndim - 1) + ((first, last),))
        total = placed if total is None else total + placed
        first += item.shape[-1]
    return total


def gather_blocks(block, axis):
    size = lax.axis_size(axis)
    return by_sender([block] + [to_ahead(block, s, axis) for s in range(1, size)], axis)


def gather_team(block):
    return gather_ahead(gather_ahead(block, "y"), "core")


def sum_team(term, tokens):
    half = term.shape[0] // 2
    term = sum_ahead([term[:half], term[half:]], "core")
    return sum_ahead([term[i : i + tokens] for i in range(0, half, tokens)], "y")


def down_routes(teams, members):
    here, before = [], []
    for member in range(members):
        for block in range(teams):
            owner = member * teams + block
            here.append((owner, block * members + member))
            if block > 0:
                before.append((owner, (block - 1) * members + member))
    return here, before


def local(
    activations,
    cotangent,
    segments,
    in_gain,
    query_gain,
    key_gain,
    post_attn_gain,
    pre_ff_gain,
    post_ff_gain,
    w_query,
    w_key,
    w_value,
    w_out,
    w_gate,
    w_up,
    w_down,
):
    all_axes = ("x", "z", "core", "y")
    teams = lax.axis_size("x") * lax.axis_size("z")
    inner = lax.axis_size("y")
    cores = lax.axis_size("core")
    members = inner * cores
    me = lax.axis_index("y")
    team = lax.axis_index("x") * lax.axis_size("z") + lax.axis_index("z")
    flat = team * members + lax.axis_index("core") * inner + me
    rows = w_query.shape[0]
    model = w_down.shape[1]
    query_cols = w_query.shape[1]
    head_dim = w_key.shape[1]
    heads = query_cols // head_dim
    qkv_cols = query_cols + 2 * head_dim
    out_rows = w_out.shape[0]
    team_rows = members * rows
    part = w_gate.shape[1] // members
    wide = -(-part // 128) * 128
    down_rows = w_down.shape[0]
    down_wide = wide // teams
    down_shift = down_wide - down_rows

    half_qkv = qkv_cols // 2
    half_out = -(-model // 256) * 128
    half = half_qkv + half_out

    def halves(qkv_block, out_block):
        out_block = jnp.pad(out_block, ((0, 0),) * (out_block.ndim - 1) + ((0, 2 * half_out - model),))
        return jnp.stack(
            [
                jnp.concatenate(
                    [
                        qkv_block[..., c * half_qkv : (c + 1) * half_qkv],
                        out_block[..., c * half_out : (c + 1) * half_out],
                    ],
                    axis=-1,
                )
                for c in range(cores)
            ]
        )

    gains = (in_gain, query_gain, key_gain, post_attn_gain, pre_ff_gain, post_ff_gain)
    gain_row = side_by_side(gains, model)[None]
    attn_rows = halves(
        jnp.concatenate([w_query, w_key, w_value], axis=1),
        jnp.concatenate([w_out, gain_row], axis=0),
    )

    def columns(weight):
        pieces = weight.reshape(rows, members, part)
        return jnp.pad(pieces, ((0, 0), (0, 0), (0, wide - part)))

    both = jnp.concatenate([columns(w_gate), columns(w_up)], axis=2).transpose(1, 0, 2)
    both = both.reshape(cores, inner, rows, 2 * wide)
    message = jnp.concatenate(
        [
            both.transpose(1, 2, 0, 3).reshape(inner, rows, cores * 2 * wide),
            jnp.broadcast_to(
                jnp.concatenate([attn_rows[c] for c in range(cores)], axis=1)[None],
                (inner, rows, cores * half),
            ),
        ],
        axis=2,
    )
    by_y = swap(message, "y")
    message = jnp.stack(
        [
            jnp.concatenate(
                [
                    by_y[:, :, c * 2 * wide : (c + 1) * 2 * wide],
                    by_y[:, :, cores * 2 * wide + c * half : cores * 2 * wide + (c + 1) * half],
                ],
                axis=2,
            )
            for c in range(cores)
        ]
    )
    by_core = swap(message, "core").reshape(members, rows, 2 * wide + half)
    by_member = by_core[:, :, : 2 * wide].reshape(team_rows, 2 * wide)
    attn_rows = by_core[:, :, 2 * wide :]
    attn_shard = jnp.concatenate(
        [
            attn_rows[:, :, :half_qkv].reshape(team_rows, half_qkv),
            jnp.concatenate(
                [
                    attn_rows[:, :out_rows, half_qkv:].reshape(members * out_rows, half_out),
                    attn_rows[:, out_rows, half_qkv:],
                ],
                axis=0,
            ),
        ],
        axis=1,
    )
    here, before = down_routes(teams, members)
    down_two = jnp.concatenate(
        [lax.ppermute(w_down, all_axes, here), lax.ppermute(w_down, all_axes, before)], axis=0
    )
    down_part = lax.dynamic_slice_in_dim(down_two, down_shift * team, down_wide, 0)
    shard = jnp.concatenate(
        [by_member, jnp.pad(down_part, ((0, team_rows - down_wide), (0, 0)))],
        axis=1,
    )
    full = lax.all_gather(shard, ("x", "z"), axis=0, tiled=True)
    full_both = full[:, : 2 * wide]
    full_down = full.reshape(teams, team_rows, -1)[:, :down_wide, 2 * wide :].reshape(wide, model)

    left = gather_axis(attn_shard[:, :half_qkv], "x", 0)
    right = gather_axis(attn_shard[:, half_qkv:], "z", 0)
    left, right, _ = lax.optimization_barrier((left, right, shard))
    left = gather_axis(left, "z", 1)
    right = gather_axis(right, "x", 0)
    left = by_sender([left, to_ahead(left, 1, "core")], "core")
    right = by_sender([right, to_ahead(right, 1, "core")], "core")
    right = right.reshape(cores, teams, team_rows, half_out)
    full_qkv = jnp.concatenate(
        [left[c].reshape(model, half_qkv) for c in range(cores)], axis=1
    )
    full_out = jnp.concatenate(
        [
            right[c, :, : members * out_rows].reshape(query_cols, half_out)
            for c in range(cores)
        ],
        axis=1,
    )[:, :model]
    gain_all = right[0, :, members * out_rows :, :128].astype(f32)
    full_gains = []
    first = 0
    for item in gains:
        size = item.shape[0]
        full_gains.append(gain_all[:, :, first : first + size].reshape(-1))
        first += size
    gain_in, gain_query, gain_key, gain_post_attn, gain_pre, gain_post = full_gains

    inputs = activations[0].astype(f32)
    segment_all = segments[0]
    tok_count = inputs.shape[0]
    first_place = me * tok_count
    place_rows = first_place + jnp.arange(tok_count, dtype=jnp.int32)
    segment_rows = lax.dynamic_slice_in_dim(segment_all, first_place, tok_count)
    earlier = jnp.sum((segment_all[None, :] < segment_rows[:, None]).astype(jnp.int32), axis=1)
    cosine, sine = rope_tables(place_rows - earlier, head_dim)
    length = segment_all.shape[0]
    key_places = (first_place + jnp.arange(length, dtype=jnp.int32)) % length
    key_segments = lax.dynamic_slice_in_dim(
        jnp.concatenate([segment_all, segment_all]), first_place, length
    )
    allowed = (segment_rows[:, None] == key_segments[None, :]) & (
        place_rows[:, None] >= key_places[None, :]
    )
    allowed = jnp.tile(allowed, (heads, 1))

    normed, in_pull = jax.vjp(rms_norm, inputs, gain_in)
    normed_low = normed.astype(bf16)
    qkv = contract(normed_low, full_qkv, 1, 0)
    query_raw = qkv[:, :query_cols].reshape(tok_count, heads, head_dim)
    key_raw = qkv[:, query_cols : query_cols + head_dim]
    value_low = qkv[:, query_cols + head_dim :].astype(bf16)

    def prepare(query_in, key_in, query_scale, key_scale):
        rotated_query = rotate(
            rms_norm(query_in, query_scale), cosine[:, None, :], sine[:, None, :]
        )
        rotated_key = rotate(rms_norm(key_in, key_scale), cosine, sine)
        return (rotated_query, rotated_key)

    (queries, key_rows), prepare_pull = jax.vjp(prepare, query_raw, key_raw, gain_query, gain_key)
    query_low = queries.astype(bf16).transpose(1, 0, 2).reshape(heads * tok_count, head_dim)
    key_value = gather_ahead(jnp.concatenate([key_rows.astype(bf16), value_low], axis=1))
    key_all = key_value[:, :head_dim]
    value_all = key_value[:, head_dim:]

    scores = contract(query_low, key_all, 1, 1) * score_scale
    scores = jnp.where(allowed, scores, far_below)
    top_score = jnp.max(scores, axis=-1, keepdims=True)
    weight = jnp.exp(scores - top_score)
    prob = weight / jnp.sum(weight, axis=-1, keepdims=True)
    prob_low = prob.astype(bf16)
    attended = contract(prob_low, value_all, 1, 0).astype(bf16)
    attended_low = attended.reshape(heads, tok_count, head_dim).transpose(1, 0, 2)
    attended_low = attended_low.reshape(tok_count, query_cols)
    attn_out = contract(attended_low, full_out, 1, 0)
    post_attn, post_attn_pull = jax.vjp(rms_norm, attn_out, gain_post_attn)
    middle = inputs + post_attn
    normed_ff, pre_pull = jax.vjp(rms_norm, middle, gain_pre)
    normed_all = gather_team(normed_ff.astype(bf16))

    gate_up = contract(normed_all, full_both, 1, 0)
    mixed, gated_pull = jax.vjp(gated_unit, gate_up[:, :wide], gate_up[:, wide:])
    mixed_low = mixed.astype(bf16)
    team_half = inner * tok_count
    branch_other = to_ahead(contract(mixed_low[team_half:], full_down, 1, 0, bf16), 1, "core")
    branch_term = contract(mixed_low[:team_half], full_down, 1, 0) + branch_other.astype(f32)
    branch_out = sum_ahead(
        [branch_term[i : i + tok_count] for i in range(0, team_half, tok_count)], "y"
    )
    post_ff, post_pull = jax.vjp(rms_norm, branch_out, gain_post)
    output = (middle + post_ff).astype(bf16)

    grad_output = cotangent[0].astype(f32)
    grad_branch, grad_post_ff = post_pull(grad_output)
    grad_branch_all = gather_team(grad_branch.astype(bf16))
    grad_mixed = contract(grad_branch_all, full_down, 1, 1)
    grad_gate, grad_up = gated_pull(grad_mixed)
    grad_both = jnp.concatenate([grad_gate.astype(bf16), grad_up.astype(bf16)], axis=1)
    grad_normed_term = contract(grad_both, full_both, 1, 1)
    grad_both, mixed_low, grad_normed_term = lax.optimization_barrier(
        (grad_both, mixed_low, grad_normed_term)
    )
    grad_normed_ff = sum_team(grad_normed_term, tok_count)
    down_term = contract(mixed_low, grad_branch_all, 0, 0, bf16)
    both_term = contract(normed_all, grad_both, 0, 0, bf16)
    ffn_terms = jnp.concatenate(
        [
            both_term.reshape(teams, team_rows, 2 * wide),
            jnp.pad(
                down_term.reshape(teams, down_wide, model),
                ((0, 0), (0, team_rows - down_wide), (0, 0)),
            ),
        ],
        axis=2,
    ).reshape(teams * team_rows, -1)
    grad_normed_ff, _ = lax.optimization_barrier((grad_normed_ff, ffn_terms))
    ffn_sum = lax.psum_scatter(ffn_terms.reshape(teams, team_rows, -1), ("x", "z"), scatter_dimension=0, tiled=True)[0]
    down_sum = ffn_sum[:down_wide, 2 * wide :]
    down_two = jnp.concatenate(
        [
            lax.ppermute(down_sum, all_axes, [(b, a) for a, b in before]),
            lax.ppermute(down_sum, all_axes, [(b, a) for a, b in here]),
        ],
        axis=0,
    )
    down_grad = lax.dynamic_slice_in_dim(
        down_two, down_wide - down_shift * (flat % teams), down_rows, 0
    ).astype(f32)

    grad_middle_add, grad_pre_ff = pre_pull(grad_normed_ff)
    grad_middle = grad_output + grad_middle_add
    grad_attn, grad_post_attn = post_attn_pull(grad_middle)
    grad_attn_low = grad_attn.astype(bf16)
    out_term = contract(attended_low, grad_attn_low, 0, 0, bf16)
    grad_attended = contract(grad_attn_low, full_out, 1, 1, bf16)
    grad_attended = grad_attended.reshape(tok_count, heads, head_dim).transpose(1, 0, 2)
    grad_attended = grad_attended.reshape(heads * tok_count, head_dim)

    grad_prob = contract(grad_attended, value_all, 1, 1)
    shift_term = jnp.sum(prob * grad_prob, axis=-1, keepdims=True)
    grad_scores = (prob * (grad_prob - shift_term)).astype(bf16)
    grad_query = contract(grad_scores, key_all, 1, 0) * score_scale
    grad_key = contract(grad_scores, query_low, 0, 0) * score_scale
    grad_value = contract(prob_low, grad_attended, 0, 0)
    grad_key_value = jnp.concatenate([grad_key, grad_value], axis=1)
    grad_key_value = sum_ahead(
        [grad_key_value[s * tok_count : (s + 1) * tok_count] for s in range(inner)]
    )
    grad_queries = grad_query.reshape(heads, tok_count, head_dim).transpose(1, 0, 2)
    grad_query_raw, grad_key_raw, grad_query_gain, grad_key_gain = prepare_pull(
        (grad_queries, grad_key_value[:, :head_dim])
    )
    grad_qkv = jnp.concatenate(
        [
            grad_query_raw.reshape(tok_count, query_cols),
            grad_key_raw,
            grad_key_value[:, head_dim:],
        ],
        axis=1,
    ).astype(bf16)
    qkv_term = contract(normed_low, grad_qkv, 0, 0, bf16)
    grad_normed = contract(grad_qkv, full_qkv, 1, 1)
    grad_input_add, grad_in_gain = in_pull(grad_normed)
    input_grad = grad_middle + grad_input_add

    grad_gains = (
        grad_in_gain,
        grad_query_gain,
        grad_key_gain,
        grad_post_attn,
        grad_pre_ff,
        grad_post_ff,
    )
    gain_terms = jnp.concatenate(
        [item.reshape(teams, members, -1) for item in grad_gains], axis=2
    ).astype(bf16)
    gain_terms = jnp.pad(gain_terms, ((0, 0), (0, 0), (0, model - gain_terms.shape[2])))
    attn_terms = halves(
        qkv_term.reshape(teams, team_rows, qkv_cols),
        jnp.concatenate(
            [out_term.reshape(teams, members * out_rows, model), gain_terms], axis=1
        ),
    )
    attn_half = reduce_axis(attn_terms, "core", 0)
    attn_half = attn_half.reshape(lax.axis_size("x"), lax.axis_size("z"), team_rows, half)
    left = reduce_axis(attn_half[..., :half_qkv], "x", 0)
    right = reduce_axis(attn_half[..., half_qkv:], "z", 1)
    left = reduce_axis(left, "z", 0)
    right = reduce_axis(right, "x", 0)
    attn_sum = jnp.concatenate(
        [
            left.reshape(members, rows, half_qkv),
            jnp.concatenate(
                [
                    right[: members * out_rows].reshape(members, out_rows, half_out),
                    right[members * out_rows :][:, None],
                ],
                axis=1,
            ),
        ],
        axis=2,
    ).reshape(cores, inner, rows, half)
    message = jnp.concatenate(
        [
            ffn_sum[:, : 2 * wide].reshape(cores, inner, rows, 2 * wide),
            attn_sum,
        ],
        axis=3,
    ).transpose(1, 0, 2, 3)
    by_y = swap(message, "y")
    attn_sum = jnp.sum(by_y[..., 2 * wide :].astype(f32), axis=0).astype(bf16)
    message = jnp.concatenate(
        [by_y[c, :, :, : 2 * wide] for c in range(inner)] + [attn_sum], axis=2
    )
    by_core = swap(message, "core").astype(f32)
    both_grad = jnp.concatenate(
        [
            by_core[c, None, :, k * 2 * wide : (k + 1) * 2 * wide]
            for c in range(cores)
            for k in range(inner)
        ],
        axis=0,
    ).transpose(1, 0, 2)
    gate_grad = both_grad[:, :, :part].reshape(rows, members * part)
    up_grad = both_grad[:, :, wide : wide + part].reshape(rows, members * part)
    attn_sum = by_core[:, :, inner * 2 * wide :]
    attn_grad = jnp.concatenate(
        [attn_sum[c, :, :half_qkv] for c in range(cores)]
        + [attn_sum[c, :, half_qkv:] for c in range(cores)],
        axis=1,
    )
    gain_grads = []
    first = qkv_cols
    for item in gains:
        size = item.shape[0]
        gain_grads.append(attn_grad[rows - 1, first : first + size])
        first += size
    return (
        output[None],
        input_grad[None],
        *gain_grads,
        attn_grad[:, :query_cols],
        attn_grad[:, query_cols : query_cols + head_dim],
        attn_grad[:, query_cols + head_dim : qkv_cols],
        attn_grad[:out_rows, qkv_cols : qkv_cols + model],
        gate_grad,
        up_grad,
        down_grad,
    )


def solution(mesh):
    fine = Mesh(mesh.devices.reshape(4, 4, 2, 4), ("x", "z", "core", "y"))
    all_axes = ("x", "z", "core", "y")
    shard = P(all_axes)
    matrix = P(all_axes, None)
    tokens = P(("x", "z", "core"), "y", None)
    return jax.shard_map(
        local,
        mesh=fine,
        in_specs=(tokens, tokens, P(("x", "z", "core"), None)) + (shard,) * 6 + (matrix,) * 7,
        out_specs=(tokens, tokens) + (shard,) * 6 + (matrix,) * 7,
        check_vma=False,
    )
```
